128 devices in a mesh: outer: 2 (over y_hi), inner: 64 (over y_lo, z, x, core).
Axes of the slice: x: 4, y: 4 (y_hi: 2, y_lo: 2; y = y_hi * 2 + y_lo), z: 4, core: 2. Of those that a mesh axis runs over, the one named last changes fastest.
Arguments:
- queries: bfloat16 [40960, 2048], P(('outer', 'inner')), may hold values from -300 to 300
- keys: bfloat16 [40960, 128], P(('outer', 'inner')), may hold values from -6 to 6
- values: bfloat16 [40960, 128], P(('outer', 'inner')), may hold values from -6 to 6
- doc_lengths: int32 [64], replicated, may hold values from 1 to 4800, 40960 in all
Outputs:
- attended: bfloat16 [40960, 2048], P(('outer', 'inner'))
The draws below stay inside these ranges and needn't reach their ends.
Inputs may be any that keep to these rules, and one draw needn't show every extreme that they name: `doc_lengths`: the lengths sum to 40960; the longest document has exactly 4800 tokens.
All inputs are finite; a program needn't handle non-finite values.
Results may differ from the reference program's by a relative error of at most 0.0036.
Values may be sent and summed in bfloat16 or wider, within the bound.
No kernel may reach another device: no remote copies, remote signals or barrier semaphores. Data moves between devices by JAX's collectives and lax.ppermute only.
A program may use at most 64 MiB of HBM per device.

```python
import math
import jax
import jax.numpy as jnp
import numpy as np
from jax import lax

HEADS = 16
HD = 128
TOK_DEV = 320
REACH = 16
TOKENS = 40960
MAXDOC = 4800
NDOCS = 64
DEVICES = 128


def shared_base(key):
    return jax.random.normal(key, (TOKENS, HD), jnp.float32)


def draw_keys(key, part):
    base = shared_base(key)
    return jnp.clip(base, -6.0, 6.0).astype(jnp.bfloat16)


def draw_queries(key, part):
    key = jax.random.fold_in(key, 23)
    drawn = jax.random.normal(key, (TOKENS, HEADS * HD), jnp.float32)
    result = jnp.clip(drawn, -6.0, 6.0)
    return jnp.clip(result, -300.0, 300.0).astype(jnp.bfloat16)


def block_scale(stream_key, dims, pieces, low, top_value):
    def one(position, blocks):
        draws = jax.random.uniform(jax.random.fold_in(jax.random.fold_in(stream_key, 6), position), (blocks,), jnp.float32, low / len(pieces), top_value / len(pieces))
        return jnp.repeat(jnp.exp(draws), dims[position] // blocks).reshape((-1,) + (1,) * (len(dims) - position - 1))

    factor_of = one(*pieces[0])
    for cut in pieces[1:]:
        factor_of = factor_of * one(*cut)
    return factor_of


def length_profile(count, total, limit, slope):
    loads = [(1 << 20) // math.isqrt(rank ** slope) + 1 for rank in range(2, count + 1)]
    spare, counts = total - limit - (count - 1), [1] * (count - 1)
    while spare > 0:
        candidates = [i for i in range(count - 1) if counts[i] < limit]
        mass, left = sum([loads[i] for i in candidates]), spare
        for i in candidates:
            extra = min(limit - counts[i], max(1, left * loads[i] // mass), spare)
            counts[i] = counts[i] + extra
            spare = spare - extra
    return np.array([limit] + counts)


def uneven_parts(own_key, count, total, limit, skew):
    if count == 2:
        one = jax.random.randint(own_key, (), max(1, total - limit), min(limit, total - 1) + 1)
        return jnp.stack([one, total - one])
    sizes = jnp.asarray(length_profile(count, total, limit, skew), jnp.int32)
    couples = (count - 1) // 2
    donor, taker = sizes[1:1 + 2 * couples:2], sizes[2:2 + 2 * couples:2]
    slack = jnp.minimum(donor - 1, limit - taker)
    shifted = jax.random.randint(jax.random.fold_in(own_key, 1), (couples,), 0, 1 << 20) % (slack + 1)
    sizes = sizes.at[1:1 + 2 * couples:2].set(donor - shifted).at[2:2 + 2 * couples:2].set(taker + shifted)
    return sizes[jax.random.permutation(jax.random.fold_in(own_key, 2), count)]


def centred(rng, dims, spread, bound, shards=(), kind=jnp.bfloat16):
    gain = block_scale(rng, dims, shards, -0.22, 0.18) if shards else 1.0
    entries = jax.random.normal(rng, dims, jnp.float32) * spread * gain
    return jnp.minimum(jnp.maximum(entries, -bound), bound).astype(kind)


def setup_inputs(seed: int = 0) -> dict:
    seeds = jax.random.split(jax.random.key(seed), 5)
    return {
        "queries": draw_queries(jax.random.fold_in(seeds[4], 71), 0),
        "keys": draw_keys(jax.random.fold_in(seeds[4], 71), 0),
        "values": centred(seeds[2], (TOKENS, HD), 1.0, 6.0, ((0, 128),)),
        "doc_lengths": uneven_parts(seeds[3], NDOCS, TOKENS, MAXDOC, 2).astype(jnp.int32),
    }


def doc_index(positions, doc_lengths):
    ends = jnp.cumsum(doc_lengths).astype(jnp.int32)
    return jnp.sum((ends[None, :] <= positions[:, None]).astype(jnp.int32), axis=1)


def attend(queries, keys, values, query_pos, key_pos, doc_lengths):
    tok_rows = queries.shape[0]
    head_size = keys.shape[1]
    heads = queries.shape[1] // head_size
    rows = queries.reshape(tok_rows * heads, head_size)
    query_doc = doc_index(query_pos, doc_lengths)
    key_doc = doc_index(key_pos, doc_lengths)
    row_pos = jnp.repeat(query_pos, heads)
    row_doc = jnp.repeat(query_doc, heads)
    block = min(1024, tok_rows * heads)
    count = tok_rows * heads // block
    scale = 1.0 / (head_size ** 0.5)

    def one_block(index):
        start = (index * block).astype(jnp.int32)
        piece = lax.dynamic_slice_in_dim(rows, start, block, 0)
        pos_piece = lax.dynamic_slice_in_dim(row_pos, start, block, 0)
        doc_piece = lax.dynamic_slice_in_dim(row_doc, start, block, 0)
        scores = lax.dot_general(piece, keys, (((1,), (1,)), ((), ())), preferred_element_type=jnp.float32) * scale
        allowed = (key_pos[None, :] <= pos_piece[:, None]) & (key_pos[None, :] >= 0) & (key_doc[None, :] == doc_piece[:, None])
        scores = jnp.where(allowed, scores, jnp.float32(-1e30))
        highest = jnp.max(scores, axis=1)
        probs = jnp.exp(scores - highest[:, None])
        total = jnp.sum(probs, axis=1)
        summed = jnp.dot(probs.astype(jnp.bfloat16), values, preferred_element_type=jnp.float32)
        return (summed / total[:, None]).astype(jnp.bfloat16)

    result = lax.map(one_block, jnp.arange(count, dtype=jnp.int32))
    return result.reshape(tok_rows, heads * head_size)


def reference(queries, keys, values, doc_lengths):
    front = (REACH - 1) * TOK_DEV
    padded_keys = jnp.concatenate([jnp.zeros((front, HD), keys.dtype), keys], axis=0)
    padded_values = jnp.concatenate([jnp.zeros((front, HD), values.dtype), values], axis=0)

    def one_device(device):
        start = (device * TOK_DEV).astype(jnp.int32)
        query_rows = lax.dynamic_slice_in_dim(queries, start, TOK_DEV, 0)
        key_rows = lax.dynamic_slice_in_dim(padded_keys, start, REACH * TOK_DEV, 0)
        value_rows = lax.dynamic_slice_in_dim(padded_values, start, REACH * TOK_DEV, 0)
        query_pos = start + jnp.arange(TOK_DEV, dtype=jnp.int32)
        key_pos = start - front + jnp.arange(REACH * TOK_DEV, dtype=jnp.int32)
        return attend(query_rows, key_rows, value_rows, query_pos, key_pos, doc_lengths)

    result = lax.map(one_device, jnp.arange(DEVICES, dtype=jnp.int32))
    return result.reshape(TOKENS, HEADS * HD)
```

```python
import functools

import jax
import jax.numpy as jnp
from jax import lax
from jax.experimental import pallas as pl
from jax.experimental.pallas import tpu as pltpu
from jax.sharding import PartitionSpec as P

AXES = ("outer", "inner")
ROW = 8
TOK = 320
HD = 128
HEADS = 16
GROUP = 4
M = GROUP * TOK
NDOCS = 64
SCALE = 1.4426950408889634 / HD**0.5
F32 = jnp.float32
BF16 = jnp.bfloat16


def permute(block, source_of):
    return lax.ppermute(block, AXES, [(source_of(i), i) for i in range(128)])


def doc_starts(doc_ref, first, last):
    def step(i, carry):
        end, a, b = carry
        end = end + doc_ref[i]
        return end, jnp.where(end <= first, end, a), jnp.where(end <= last, end, b)

    zero = jnp.int32(0)
    _, a, b = lax.fori_loop(0, NDOCS, step, (zero, zero, zero))
    return a, b


def stack_heads(q_ref):
    return jnp.concatenate([q_ref[:, i * HD : (i + 1) * HD] for i in range(GROUP)], 0)


def scores_t(k, q):
    return lax.dot_general(k, q, (((1,), (1,)), ((), ())), preferred_element_type=F32)


def weigh(v, p):
    return lax.dot_general(
        v, p.astype(BF16), (((0,), (0,)), ((), ())), preferred_element_type=F32
    )


def fold(p):
    return functools.reduce(lambda a, b: a + b, [p[i : i + 8] for i in range(0, p.shape[0], 8)])


def own_kernel(info, docs, q_ref, kv_ref, acc_ref, tot_ref, m_ref, start_ref):
    token = lax.broadcasted_iota(jnp.int32, (1, TOK), 1)

    @pl.when(pl.program_id(0) == 0)
    def _():
        base = info[0] * TOK

        def step(i, carry):
            end, begin = carry
            end = end + docs[i]
            return end, jnp.where(end <= token, end, begin)

        low = jnp.full((1, TOK), -(1 << 20), jnp.int32)
        _, begin = lax.fori_loop(0, NDOCS, step, (-base, jnp.maximum(low, -base)))
        start_ref[...] = jnp.concatenate([begin] * GROUP, 1)

    q = stack_heads(q_ref)
    s = scores_t(kv_ref[:TOK], q) * SCALE
    key = lax.broadcasted_iota(jnp.int32, (TOK, M), 0)
    row = jnp.concatenate([token] * GROUP, 1)
    s = jnp.where((key <= row) & (key >= start_ref[...]), s, F32(-1e30))
    m = jnp.max(s, 0, keepdims=True)
    p = jnp.exp2(s - m)
    m_ref[...] = m
    tot_ref[...] = fold(p)
    acc_ref[...] = weigh(kv_ref[TOK:], p)


def add_blocks(q, blocks, m, start, masked):
    k = jnp.concatenate([b[0] for b in blocks], 0)
    v = jnp.concatenate([b[1] for b in blocks], 0)
    p = jnp.exp2(scores_t(k, q) * SCALE - m)
    if masked:
        key = lax.broadcasted_iota(jnp.int32, (TOK, M), 0)
        keep = [key >= start - b[2] for b in blocks]
        p = jnp.where(jnp.concatenate(keep, 0), p, F32(0))
    return weigh(v, p), fold(p)


def span(ref, *at):
    return ref[(*at, slice(0, TOK))], ref[(*at, slice(TOK, 2 * TOK))]


def three_blocks(core, z_ref, zo_ref):
    side = (1 - 2 * core) * TOK
    return [
        (*span(z_ref), -8 * TOK),
        (*span(zo_ref, 0), -8 * TOK + side),
        (*span(zo_ref, 1), jnp.where(core == 0, -15 * TOK, -TOK)),
    ]


def four_blocks(core, shift, wrap, x_ref, xo_ref):
    side = (1 - 2 * core) * TOK
    near = -2 * shift * TOK
    far = near - 8 * TOK
    at = 1 - wrap
    return [
        (*span(x_ref, at), near),
        (*span(xo_ref, at), near + side),
        (*span(x_ref, wrap), far),
        (*span(xo_ref, wrap), far + side),
    ]


def chunk(q, blocks, state, m, start, first, last, near=None):
    acc_in, tot_in, acc_out, tot_out = state
    lowest = functools.reduce(jnp.minimum, [b[2] for b in blocks])
    highest = functools.reduce(jnp.maximum, [b[2] for b in blocks]) + TOK - 1
    full = last <= lowest
    if near is None:
        some = first <= highest
    else:
        some = first <= functools.reduce(jnp.maximum, [b[2] for b in blocks[near:]]) + TOK - 1

    def put(part, masked):
        acc, tot = add_blocks(q, part, m, start, masked)
        acc_out[...] = acc_in[...] + acc
        tot_out[...] = tot_in[...] + tot

    @pl.when(full)
    def _():
        put(blocks, False)

    @pl.when(jnp.logical_not(full) & some)
    def _():
        put(blocks, True)

    rest = jnp.logical_not(full) & jnp.logical_not(some)
    if near is not None:
        few = rest & (first <= highest)
        rest = rest & (first > highest)

        @pl.when(few)
        def _():
            put(blocks[:near], True)

    @pl.when(rest)
    def _():
        acc_out[...] = acc_in[...]
        tot_out[...] = tot_in[...]


def bounds(info, docs):
    base = info[0] * TOK
    first, last = doc_starts(docs, base, base + TOK - 1)
    return first - base, last - base


def z_kernel(info, docs, q_ref, z_ref, zo_ref, m_ref, start_ref, acc_in, tot_in, acc, tot):
    first, last = bounds(info, docs)
    blocks = three_blocks(info[1], z_ref, zo_ref)
    state = (acc_in, tot_in, acc, tot)
    chunk(stack_heads(q_ref), blocks, state, m_ref[...], start_ref[...], first, last)


def x_kernel(shift, info, docs, q_ref, x_ref, xo_ref, m_ref, start_ref, acc_in, tot_in, acc, tot):
    first, last = bounds(info, docs)
    blocks = four_blocks(info[1], shift, info[1 + shift], x_ref, xo_ref)
    state = (acc_in, tot_in, acc, tot)
    chunk(stack_heads(q_ref), blocks, state, m_ref[...], start_ref[...], first, last, near=2)


def last_kernel(
    shift, info, docs, q_ref, x_ref, xo_ref, m_ref, start_ref, acc_in, tot_in, *rest
):
    sources, (out_ref, acc, tot, window, sem) = rest[:-5], rest[-5:]
    first, last = bounds(info, docs)
    q = stack_heads(q_ref)
    core = info[1]
    blocks = four_blocks(core, shift, info[1 + shift], x_ref, xo_ref)
    state = (acc_in, tot_in, acc, tot)
    chunk(q, blocks, state, m_ref[...], start_ref[...], first, last, near=2)

    total = jnp.sum(tot[...], 0, keepdims=True)

    def put(result):
        for i in range(GROUP):
            part = result[:, i * TOK : (i + 1) * TOK].T
            out_ref[:, i * HD : (i + 1) * HD] = part.astype(BF16)

    put(acc[...] / total)

    @pl.when(jnp.logical_not(jnp.max(total) < F32(1e30)))
    def _():
        kv, z, zo, xs, xos = sources
        side = jnp.where(core == 0, 1, -1)
        pieces = [(kv, 0), (z, -8), (zo.at[0], side - 8), (zo.at[1], jnp.where(core == 0, -15, -1))]
        for s, x, xo in zip((1, 3, 2), xs, xos):
            wrap = info[1 + s]
            for half in (0, 1):
                far = jnp.where(wrap == half, -8, 0)
                pieces += [(x.at[half], far - 2 * s), (xo.at[half], far - 2 * s + side)]
        for piece, place in pieces:
            copy = pltpu.make_async_copy(piece, window.at[place + 15], sem)
            copy.start()
            copy.wait()

        row = jnp.concatenate([lax.broadcasted_iota(jnp.int32, (1, TOK), 1)] * GROUP, 1)

        def step(i, carry):
            top, acc_c, tot_c = carry
            block = 15 - i
            s = scores_t(window[block, :TOK], q) * SCALE
            key = lax.broadcasted_iota(jnp.int32, (TOK, M), 0) + (block - 15) * TOK
            keep = (key <= row) & (key >= start_ref[...])
            s = jnp.where(keep, s, F32(-1e30))
            new = jnp.maximum(top, jnp.max(s, 0, keepdims=True))
            p = jnp.where(keep, jnp.exp2(s - new), F32(0))
            decay = jnp.exp2(top - new)
            return new, acc_c * decay + weigh(window[block, TOK:], p), tot_c * decay + fold(p)

        zero = (jnp.full((1, M), -1e30, F32), jnp.zeros((HD, M), F32), jnp.zeros((8, M), F32))
        _, acc_c, tot_c = lax.fori_loop(0, 16, step, zero)
        put(acc_c / jnp.sum(tot_c, 0, keepdims=True))


def flat(kernel):
    def wrapped(info, docs, q, x, xo, m, start, acc_in, tot_in, *rest):
        refs = list(rest)
        sources = [refs[0], refs[1], refs[2], refs[3:6], refs[6:9]]
        return kernel(info, docs, q, x, xo, m, start, acc_in, tot_in, *sources, *refs[9:])

    return wrapped


SMEM = pl.BlockSpec(memory_space=pltpu.SMEM)
Q_SPEC = pl.BlockSpec((TOK, GROUP * HD), lambda g: (0, g))
ACC_SPEC = pl.BlockSpec((HD, M), lambda g: (0, g))
TOT_SPEC = pl.BlockSpec((8, M), lambda g: (0, g))
M_SPEC = pl.BlockSpec((1, M), lambda g: (0, g))
START_SPEC = pl.BlockSpec((1, M), lambda g: (0, 0))
ANY = pl.BlockSpec(memory_space=pl.ANY)
ACC = jax.ShapeDtypeStruct((HD, HEADS * TOK), F32)
TOT = jax.ShapeDtypeStruct((8, HEADS * TOK), F32)


def whole(array):
    return pl.BlockSpec(array.shape, lambda g: (0,) * array.ndim)


def cost(keys):
    rows = HEADS * TOK
    return pl.CostEstimate(
        flops=4 * rows * keys * HD, bytes_accessed=8 * 2**20, transcendentals=rows * keys
    )


PARAMS = pltpu.CompilerParams(
    vmem_limit_bytes=56 * 2**20, dimension_semantics=("arbitrary",)
)


def shards(queries, keys, values, doc_lengths):
    device = lax.axis_index(AXES)
    core = device % 2
    col = device % ROW // 2
    info = jnp.stack([device, core] + [(col < s).astype(jnp.int32) for s in (1, 2, 3)])
    info = info.astype(jnp.int32)
    own = jnp.concatenate([keys, values], 0)

    z1 = permute(own, lambda i: (i - ROW) % 128)
    z2 = permute(own, lambda i: (i - 2 * ROW) % 128)

    grid = (HEADS // GROUP,)
    acc, tot, m, start = pl.pallas_call(
        own_kernel,
        grid=grid,
        out_shape=(
            ACC,
            TOT,
            jax.ShapeDtypeStruct((1, HEADS * TOK), F32),
            jax.ShapeDtypeStruct((1, M), jnp.int32),
        ),
        in_specs=[SMEM, SMEM, Q_SPEC, whole(own)],
        out_specs=(ACC_SPEC, TOT_SPEC, M_SPEC, START_SPEC),
        compiler_params=PARAMS,
        cost_estimate=cost(TOK),
        name="own",
    )(info, doc_lengths, queries, own)

    z_other = permute(jnp.stack([z1, jnp.where(core == 0, own, z2)]), lambda i: i ^ 1)
    xs, xos = [], []
    for s in (1, 3, 2):
        message = jnp.stack([z1, jnp.where(col + s < 4, own, z2)])
        got = permute(message, lambda i: i // ROW * ROW + (i % ROW - 2 * s) % ROW)
        xs.append(got)
    for got in xs:
        xos.append(permute(got, lambda i: i ^ 1))

    acc, tot = pl.pallas_call(
        z_kernel,
        grid=grid,
        out_shape=(ACC, TOT),
        in_specs=[SMEM, SMEM, Q_SPEC, whole(z1), whole(z_other), M_SPEC, START_SPEC, ACC_SPEC, TOT_SPEC],
        out_specs=(ACC_SPEC, TOT_SPEC),
        input_output_aliases={7: 0, 8: 1},
        compiler_params=PARAMS,
        cost_estimate=cost(3 * TOK),
        name="zpart",
    )(info, doc_lengths, queries, z1, z_other, m, start, acc, tot)

    for s, x, xo in list(zip((1, 3, 2), xs, xos))[:2]:
        acc, tot = pl.pallas_call(
            functools.partial(x_kernel, s),
            grid=grid,
            out_shape=(ACC, TOT),
            in_specs=[SMEM, SMEM, Q_SPEC, whole(x), whole(xo), M_SPEC, START_SPEC, ACC_SPEC, TOT_SPEC],
            out_specs=(ACC_SPEC, TOT_SPEC),
            input_output_aliases={7: 0, 8: 1},
            compiler_params=PARAMS,
            cost_estimate=cost(4 * TOK),
            name="xpart",
        )(info, doc_lengths, queries, x, xo, m, start, acc, tot)

    x, xo = xs[2], xos[2]
    return pl.pallas_call(
        flat(functools.partial(last_kernel, 2)),
        grid=grid,
        out_shape=jax.ShapeDtypeStruct(queries.shape, BF16),
        in_specs=[SMEM, SMEM, Q_SPEC, whole(x), whole(xo), M_SPEC, START_SPEC, ACC_SPEC, TOT_SPEC]
        + [ANY] * 9,
        out_specs=Q_SPEC,
        scratch_shapes=[
            pltpu.VMEM((HD, M), F32),
            pltpu.VMEM((8, M), F32),
            pltpu.VMEM((16, 2 * TOK, HD), BF16),
            pltpu.SemaphoreType.DMA,
        ],
        compiler_params=PARAMS,
        cost_estimate=cost(4 * TOK),
        name="lastpart",
    )(info, doc_lengths, queries, x, xo, m, start, acc, tot, own, z1, z_other, *xs, *xos)


def solution(mesh):
    rows = P(AXES, None)
    return jax.shard_map(
        shards, mesh=mesh, in_specs=(rows, rows, rows, P()), out_specs=rows, check_vma=False
    )
```

```python
import functools

import jax
import jax.numpy as jnp
from jax import lax
from jax.experimental import pallas as pl
from jax.experimental.pallas import tpu as pltpu
from jax.sharding import PartitionSpec as P

AXES = ("outer", "inner")
ROW = 8
TOK = 320
HD = 128
HEADS = 16
GROUP = 4
GROUPS = HEADS // GROUP
M = GROUP * TOK
NDOCS = 64
DEVICES = 128
SCALE = 1.4426950408889634 / HD**0.5
NEVER = -1e30
F32 = jnp.float32
BF16 = jnp.bfloat16
MIB = 2**20


def place():
    device = lax.axis_index("outer") * 64 + lax.axis_index("inner")
    return device, lax.rem(device, 2)


def columns(g, width=M):
    return pl.ds(pl.multiple_of(g * width, width), width)


def dot(a, b):
    return jnp.dot(a, b, preferred_element_type=F32)


def fold(p):
    return functools.reduce(lambda a, b: a + b, [p[i : i + 8] for i in range(0, p.shape[0], 8)])


def causal(begin):
    key = lax.broadcasted_iota(jnp.int32, (TOK, TOK), 0)
    row = lax.broadcasted_iota(jnp.int32, (TOK, TOK), 1)
    return jnp.where((key <= row) & (key >= begin), F32(0), F32(NEVER))


def own_kernel(docs, q_ref, kv_ref, qt_ref, acc_ref, tot_ref, begin_ref, first_ref, bias_ref):
    device, _ = place()
    token = lax.broadcasted_iota(jnp.int32, (1, TOK), 1)
    end = -device * TOK
    first = end
    begin = jnp.full((1, TOK), end, jnp.int32)
    for i in range(NDOCS):
        end = end + docs[i]
        begin = jnp.where(end <= token, end, begin)
        first = jnp.where(end <= 0, end, first)
    first_ref[0] = first
    begin_ref[...] = jnp.concatenate([begin] * GROUP, 1)
    bias_ref[...] = jnp.concatenate([causal(begin)] * GROUP, 1)
    qt_ref[HD:, :] = jnp.zeros((HD, HEADS * TOK), BF16)
    k = kv_ref[:TOK]
    vt = kv_ref[TOK:].T

    @pl.loop(0, GROUPS)
    def _(g):
        heads = [q_ref[:, columns(g * GROUP + i, HD)] for i in range(GROUP)]
        qt = jnp.concatenate(heads, 0).T
        qt_ref[:HD, columns(g)] = qt
        s = dot(k, qt) + bias_ref[...]
        m = jnp.max(s, 0, keepdims=True).astype(BF16).astype(F32)
        p = jnp.exp2((s - m) * SCALE)
        tot_ref[:, columns(g)] = fold(p)
        acc_ref[:, columns(g)] = dot(vt, p.astype(BF16))
        shift = jnp.where(begin_ref[...] < 0, -m, F32(NEVER))
        line = lax.broadcasted_iota(jnp.int32, (16, M), 0)
        extra = jnp.where(line == 0, shift, jnp.where(line == 1, F32(1), F32(0)))
        qt_ref[HD : HD + 16, columns(g)] = extra.astype(BF16)


def fill(blocks, first, k_ref, vt_ref):
    for i, (block, position) in enumerate(blocks):
        rows = slice(i * TOK, (i + 1) * TOK)
        k_ref[rows, :HD] = block[:TOK]
        key = lax.broadcasted_iota(jnp.int32, (TOK, HD), 0) + position
        lane = lax.broadcasted_iota(jnp.int32, (TOK, HD), 1)
        late = jnp.where(key >= first, F32(0), F32(NEVER))
        bias = jnp.where(lane == 0, F32(1), jnp.where(lane == 1, late, F32(0)))
        k_ref[rows, HD:] = bias.astype(BF16)
    vt_ref[...] = jnp.concatenate([block[TOK:] for block, _ in blocks], 0).T


def pair(ours, theirs, step, side):
    return [(ours, step * TOK), (theirs, (step + side) * TOK)]


def partial(g, qt_ref, k_ref, vt_ref):
    p = jnp.exp2(dot(k_ref[...], qt_ref[:, columns(g)]) * SCALE)
    return dot(vt_ref[...], p.astype(BF16)), fold(p)


def middle_kernel(steps, first_ref, qt_ref, ours, theirs, acc_in, tot_in, acc, tot, k_ref, vt_ref):
    _, core = place()
    side = 1 - 2 * core
    first = first_ref[0]

    @pl.when(first < (max(steps) + 2) * TOK)
    def _():
        blocks = []
        for i, step in enumerate(steps):
            at = pl.ds(i * 2 * TOK, 2 * TOK)
            blocks += pair(ours.at[at], theirs.at[at], step, side)
        fill(blocks, first, k_ref, vt_ref)

        @pl.loop(0, GROUPS)
        def _(g):
            a, t = partial(g, qt_ref, k_ref, vt_ref)
            acc[:, columns(g)] = acc_in[:, columns(g)] + a
            tot[:, columns(g)] = tot_in[:, columns(g)] + t


def last_kernel(
    first_ref, qt_ref, x_ref, far, far2, near, near2, z, z2, own, begin_ref, acc, tot,
    out_hbm, k_ref, vt_ref, out_ref, window, sems,
):
    _, core = place()
    side = 1 - 2 * core
    first = first_ref[0]
    x_step = jnp.where(core == 0, -15, -1)
    blocks = [(x_ref, x_step * TOK)]
    for i, step in enumerate((-10, -12, -14)):
        at = pl.ds(i * 2 * TOK, 2 * TOK)
        blocks += pair(far.at[at], far2.at[at], step, side)
    some = first < jnp.where(core == 0, -8, 0) * TOK

    @pl.when(some)
    def _():
        fill(blocks, first, k_ref, vt_ref)

    def send(g):
        return pltpu.make_async_copy(
            out_ref.at[lax.rem(g, 2)], out_hbm.at[:, columns(g, GROUP * HD)], sems.at[lax.rem(g, 2)]
        )

    def put(g, result):
        for i in range(GROUP):
            part = result[:, i * TOK : (i + 1) * TOK].T
            out_ref[lax.rem(g, 2), :, i * HD : (i + 1) * HD] = part.astype(BF16)

    @pl.loop(0, GROUPS)
    def _(g):
        @pl.when(g >= 2)
        def _():
            send(g - 2).wait()

        def finish(a, t):
            total = jnp.sum(t, 0, keepdims=True)
            put(g, a / total)
            return jnp.max(total)

        def with_blocks():
            a, t = partial(g, qt_ref, k_ref, vt_ref)
            return finish(acc[:, columns(g)] + a, tot[:, columns(g)] + t)

        def without():
            return finish(acc[:, columns(g)], tot[:, columns(g)])

        largest = lax.cond(some, with_blocks, without)

        @pl.when(jnp.logical_not(largest < F32(1e30)))
        def _():
            pieces = [(own, 0), (x_ref, x_step), (z, -8), (z2, side - 8)]
            for i in range(3):
                at = pl.ds(i * 2 * TOK, 2 * TOK)
                pieces += [(near.at[at], -2 - 2 * i), (near2.at[at], side - 2 - 2 * i)]
                pieces += [(far.at[at], -10 - 2 * i), (far2.at[at], side - 10 - 2 * i)]
            for piece, step in pieces:
                window[step + 15] = piece[...]
            q = qt_ref[:HD, columns(g)]
            row = jnp.concatenate([lax.broadcasted_iota(jnp.int32, (1, TOK), 1)] * GROUP, 1)

            def step(i, carry):
                top, a, t = carry
                s = dot(window[15 - i, :TOK], q) * SCALE
                key = lax.broadcasted_iota(jnp.int32, (TOK, M), 0) - i * TOK
                keep = (key <= row) & (key >= begin_ref[...])
                s = jnp.where(keep, s, F32(NEVER))
                new = jnp.maximum(top, jnp.max(s, 0, keepdims=True))
                p = jnp.where(keep, jnp.exp2(s - new), F32(0))
                decay = jnp.exp2(top - new)
                return new, a * decay + dot(window[15 - i, TOK:].T, p.astype(BF16)), t * decay + fold(p)

            zero = (jnp.full((1, M), NEVER, F32), jnp.zeros((HD, M), F32), jnp.zeros((8, M), F32))
            _, a, t = lax.fori_loop(0, 16, step, zero)
            put(g, a / jnp.sum(t, 0, keepdims=True))

        send(g).start()

    for g in (GROUPS - 2, GROUPS - 1):
        send(g).wait()


VMEM = pl.BlockSpec(memory_space=pltpu.VMEM)
SMEM = pl.BlockSpec(memory_space=pltpu.SMEM)
QT = pltpu.VMEM((2 * HD, HEADS * TOK), BF16)
ACC = pltpu.VMEM((HD, HEADS * TOK), F32)
TOT = pltpu.VMEM((8, HEADS * TOK), F32)


def params(mib):
    return pltpu.CompilerParams(vmem_limit_bytes=mib * MIB)


def cost(keys):
    rows = HEADS * TOK
    return pl.CostEstimate(
        flops=8 * rows * keys * HD, bytes_accessed=MIB, transcendentals=rows * keys
    )


def layout(keys):
    return [pltpu.VMEM((keys, 2 * HD), BF16), pltpu.VMEM((HD, keys), BF16)]


def chip(array):
    return pltpu.with_memory_space_constraint(array, pltpu.VMEM)


def permute(block, pairs):
    return lax.ppermute(block, AXES, pairs)


def shift_row(block):
    return permute(block, [(i, i + ROW) for i in range(DEVICES - ROW)])


def swap(block):
    return permute(block, [(i, i ^ 1) for i in range(DEVICES)])


def own_part(queries, own, doc_lengths):
    return pl.pallas_call(
        own_kernel,
        out_shape=(
            QT, ACC, TOT, pltpu.VMEM((1, M), jnp.int32), jax.ShapeDtypeStruct((1,), jnp.int32)
        ),
        in_specs=[SMEM, VMEM, VMEM],
        out_specs=(VMEM, VMEM, VMEM, VMEM, SMEM),
        scratch_shapes=[pltpu.VMEM((TOK, M), F32)],
        compiler_params=params(16),
        cost_estimate=cost(TOK),
        name="own",
    )(doc_lengths, chip(queries), chip(own))


def middle_part(steps, first, qt, ours, theirs, acc, tot):
    keys = 2 * TOK * len(steps)
    return pl.pallas_call(
        functools.partial(middle_kernel, steps),
        out_shape=(ACC, TOT),
        in_specs=[SMEM] + [VMEM] * 5,
        out_specs=(VMEM, VMEM),
        scratch_shapes=layout(keys),
        input_output_aliases={4: 0, 5: 1},
        compiler_params=params(28),
        cost_estimate=cost(keys),
        name="middle",
    )(first, *[chip(x) for x in (qt, ours, theirs, acc, tot)])


def last_part(first, arrays, shape):
    return pl.pallas_call(
        last_kernel,
        out_shape=jax.ShapeDtypeStruct(shape, BF16),
        in_specs=[SMEM] + [VMEM] * len(arrays),
        out_specs=pl.BlockSpec(memory_space=pl.ANY),
        scratch_shapes=layout(7 * TOK)
        + [
            pltpu.VMEM((2, TOK, GROUP * HD), BF16),
            pltpu.VMEM((16, 2 * TOK, HD), BF16),
            pltpu.SemaphoreType.DMA((2,)),
        ],
        compiler_params=params(36),
        cost_estimate=cost(7 * TOK),
        name="last",
    )(first, *[chip(x) for x in arrays])


def shards(queries, keys, values, doc_lengths):
    col = lax.axis_index("inner") % ROW // 2
    own = jnp.concatenate([keys, values], 0)

    z = shift_row(own)
    x = permute(own, [(i, i + 1) for i in range(0, DEVICES, 2)]
                + [(i, i + 15) for i in range(1, DEVICES - 15, 2)])
    qt, acc, tot, begin, first = own_part(queries, own, doc_lengths)
    z, acc, tot = lax.optimization_barrier((z, acc, tot))

    near = []
    for s in (1, 2, 3):
        message = jnp.where(col + s < ROW // 2, own, z)
        route = [(i, i // ROW * ROW + (i + 2 * s) % ROW) for i in range(DEVICES)]
        near.append(permute(message, route))
    z2 = swap(z)
    acc, tot = middle_part((-8,), first, qt, z, z2, acc, tot)

    near = jnp.concatenate(near, 0)
    far = shift_row(near)
    near2 = swap(near)
    acc, tot = middle_part((-2, -4, -6), first, qt, near, near2, acc, tot)
    far2 = swap(far)
    arrays = (qt, x, far, far2, near, near2, z, z2, own, begin, acc, tot)
    return last_part(first, arrays, queries.shape)


def solution(mesh):
    rows = P(AXES, None)
    return jax.shard_map(
        shards, mesh=mesh, in_specs=(rows, rows, rows, P()), out_specs=rows, check_vma=False
    )
```

```python
import functools

import jax
import jax.numpy as jnp
from jax import lax
from jax.experimental import pallas as pl
from jax.experimental.pallas import tpu as pltpu
from jax.sharding import PartitionSpec as P

AXES = ("outer", "inner")
ROW = 8
TOK = 320
HD = 128
HEADS = 16
GROUP = 4
GROUPS = HEADS // GROUP
M = GROUP * TOK
NDOCS = 64
DEVICES = 128
SCALE = 1.4426950408889634 / HD**0.5
NEVER = -1e30
F32 = jnp.float32
BF16 = jnp.bfloat16
MIB = 2**20


def place():
    device = lax.axis_index("outer") * 64 + lax.axis_index("inner")
    return device, lax.rem(device, 2)


def columns(g, width=M):
    return pl.ds(g * width if isinstance(g, int) else pl.multiple_of(g * width, width), width)


def dot(a, b):
    return jnp.dot(a, b, preferred_element_type=F32)


def fold(p):
    return functools.reduce(lambda a, b: a + b, [p[i : i + 8] for i in range(0, p.shape[0], 8)])


def causal(begin):
    key = lax.broadcasted_iota(jnp.int32, (TOK, TOK), 0)
    row = lax.broadcasted_iota(jnp.int32, (TOK, TOK), 1)
    return jnp.where((key <= row) & (key >= begin), F32(0), F32(NEVER))


def pack_kernel(k_hbm, v_hbm, kv_ref, sems):
    copies = [
        pltpu.make_async_copy(half, kv_ref.at[pl.ds(i * TOK, TOK)], sems.at[i])
        for i, half in enumerate((k_hbm, v_hbm))
    ]
    for copy in copies:
        copy.start()
    for copy in copies:
        copy.wait()


def own_kernel(
    docs_hbm, q_hbm, kv_ref, qt_ref, acc_ref, tot_ref, begin_ref, first_ref,
    bias_ref, q_ref, docs, sems, docs_sem,
):
    read_docs = pltpu.make_async_copy(docs_hbm, docs, docs_sem)
    read_docs.start()

    def read(g):
        wide = columns(g, GROUP * HD)
        return pltpu.make_async_copy(q_hbm.at[:, wide], q_ref.at[:, wide], sems.at[g])

    for g in range(GROUPS):
        read(g).start()
    read_docs.wait()
    device, _ = place()
    token = lax.broadcasted_iota(jnp.int32, (1, TOK), 1)
    end = -device * TOK
    first = end
    begin = jnp.full((1, TOK), end, jnp.int32)
    for i in range(NDOCS):
        end = end + docs[i]
        begin = jnp.where(end <= token, end, begin)
        first = jnp.where(end <= 0, end, first)
    first_ref[0] = first
    begin_ref[...] = jnp.concatenate([begin] * GROUP, 1)
    bias_ref[...] = jnp.concatenate([causal(begin)] * GROUP, 1)
    qt_ref[HD:, :] = jnp.zeros((HD, HEADS * TOK), BF16)
    k = kv_ref[:TOK]
    vt = kv_ref[TOK:].T

    @pl.loop(0, GROUPS)
    def _(g):
        read(g).wait()
        heads = [q_ref[:, columns(g * GROUP + i, HD)] for i in range(GROUP)]
        qt = jnp.concatenate(heads, 0).T
        qt_ref[:HD, columns(g)] = qt
        s = dot(k, qt) + bias_ref[...]
        m = jnp.max(s, 0, keepdims=True)
        p = jnp.exp2((s - m) * SCALE)
        tot_ref[:, columns(g)] = fold(p)
        acc_ref[:, columns(g)] = dot(vt, p.astype(BF16))
        shift = jnp.where(begin_ref[...] < 0, -m, F32(NEVER))
        line = lax.broadcasted_iota(jnp.int32, (16, M), 0)
        extra = jnp.where(line == 3, F32(1), F32(0))
        for i in range(3):
            part = shift.astype(BF16).astype(F32)
            extra = jnp.where(line == i, part, extra)
            shift = shift - part
        qt_ref[HD : HD + 16, columns(g)] = extra.astype(BF16)


def fill(blocks, first, k_ref, vt_ref):
    for i, (block, position) in enumerate(blocks):
        rows = slice(i * TOK, (i + 1) * TOK)
        k_ref[rows, :HD] = block[:TOK]
        key = lax.broadcasted_iota(jnp.int32, (TOK, HD), 0) + position
        lane = lax.broadcasted_iota(jnp.int32, (TOK, HD), 1)
        late = jnp.where(key >= first, F32(0), F32(NEVER))
        bias = jnp.where(lane < 3, F32(1), jnp.where(lane == 3, late, F32(0)))
        k_ref[rows, HD:] = bias.astype(BF16)
    vt_ref[...] = jnp.concatenate([block[TOK:] for block, _ in blocks], 0).T


def pair(ours, theirs, step, side):
    return [(ours, step * TOK), (theirs, (step + side) * TOK)]


def partial(g, qt_ref, k_ref, vt_ref):
    p = jnp.exp2(dot(k_ref[...], qt_ref[:, columns(g)]) * SCALE)
    return dot(vt_ref[...], p.astype(BF16)), fold(p)


def add_all(first, top, blocks, qt_ref, acc_in, tot_in, acc, tot, k_ref, vt_ref):
    @pl.when(first < top)
    def _():
        fill(blocks, first, k_ref, vt_ref)

        @pl.loop(0, GROUPS)
        def _(g):
            a, t = partial(g, qt_ref, k_ref, vt_ref)
            acc[:, columns(g)] = acc_in[:, columns(g)] + a
            tot[:, columns(g)] = tot_in[:, columns(g)] + t


def z_kernel(first_ref, qt_ref, z, z2, x_ref, *state):
    _, core = place()
    blocks = pair(z, z2, -8, 1 - 2 * core)
    blocks.append((x_ref, jnp.where(core == 0, -15, -1) * TOK))
    add_all(first_ref[0], jnp.where(core == 0, -6, 0) * TOK, blocks, qt_ref, *state)


def near_kernel(first_ref, qt_ref, near, near2, *state):
    _, core = place()
    blocks = []
    for i, step in enumerate((-2, -4, -6)):
        at = pl.ds(i * 2 * TOK, 2 * TOK)
        blocks += pair(near.at[at], near2.at[at], step, 1 - 2 * core)
    add_all(first_ref[0], 0, blocks, qt_ref, *state)


def last_kernel(
    first_ref, qt_ref, x_ref, far, far2, near, near2, z, z2, own, begin_ref, acc, tot,
    out_hbm, k_ref, vt_ref, out_ref, window, sems,
):
    _, core = place()
    side = 1 - 2 * core
    first = first_ref[0]
    x_step = jnp.where(core == 0, -15, -1)
    blocks = []
    for i, step in enumerate((-10, -12, -14)):
        at = pl.ds(i * 2 * TOK, 2 * TOK)
        blocks += pair(far.at[at], far2.at[at], step, side)
    some = first < -8 * TOK

    @pl.when(some)
    def _():
        fill(blocks, first, k_ref, vt_ref)

    def send(g):
        return pltpu.make_async_copy(
            out_ref.at[lax.rem(g, 2)], out_hbm.at[:, columns(g, GROUP * HD)], sems.at[lax.rem(g, 2)]
        )

    def put(g, result):
        for i in range(GROUP):
            part = result[:, i * TOK : (i + 1) * TOK].T
            out_ref[lax.rem(g, 2), :, i * HD : (i + 1) * HD] = part.astype(BF16)

    @pl.loop(0, GROUPS)
    def _(g):
        @pl.when(g >= 2)
        def _():
            send(g - 2).wait()

        def finish(a, t):
            total = jnp.sum(t, 0, keepdims=True)
            put(g, a / total)
            return jnp.max(total)

        def with_blocks():
            a, t = partial(g, qt_ref, k_ref, vt_ref)
            return finish(acc[:, columns(g)] + a, tot[:, columns(g)] + t)

        def without():
            return finish(acc[:, columns(g)], tot[:, columns(g)])

        largest = lax.cond(some, with_blocks, without)

        @pl.when(jnp.logical_not(largest < F32(1e30)))
        def _():
            pieces = [(own, 0), (x_ref, x_step), (z, -8), (z2, side - 8)]
            for i in range(3):
                at = pl.ds(i * 2 * TOK, 2 * TOK)
                pieces += [(near.at[at], -2 - 2 * i), (near2.at[at], side - 2 - 2 * i)]
                pieces += [(far.at[at], -10 - 2 * i), (far2.at[at], side - 10 - 2 * i)]
            for piece, step in pieces:
                window[step + 15] = piece[...]
            q = qt_ref[:HD, columns(g)]
            row = jnp.concatenate([lax.broadcasted_iota(jnp.int32, (1, TOK), 1)] * GROUP, 1)

            def step(i, carry):
                top, a, t = carry
                s = dot(window[15 - i, :TOK], q) * SCALE
                key = lax.broadcasted_iota(jnp.int32, (TOK, M), 0) - i * TOK
                keep = (key <= row) & (key >= begin_ref[...])
                s = jnp.where(keep, s, F32(NEVER))
                new = jnp.maximum(top, jnp.max(s, 0, keepdims=True))
                p = jnp.where(keep, jnp.exp2(s - new), F32(0))
                decay = jnp.exp2(top - new)
                return new, a * decay + dot(window[15 - i, TOK:].T, p.astype(BF16)), t * decay + fold(p)

            zero = (jnp.full((1, M), NEVER, F32), jnp.zeros((HD, M), F32), jnp.zeros((8, M), F32))
            _, a, t = lax.fori_loop(0, 16, step, zero)
            put(g, a / jnp.sum(t, 0, keepdims=True))

        send(g).start()

    for g in (GROUPS - 2, GROUPS - 1):
        send(g).wait()


VMEM = pl.BlockSpec(memory_space=pltpu.VMEM)
SMEM = pl.BlockSpec(memory_space=pltpu.SMEM)
ANY = pl.BlockSpec(memory_space=pl.ANY)
QT = pltpu.VMEM((2 * HD, HEADS * TOK), BF16)
ACC = pltpu.VMEM((HD, HEADS * TOK), F32)
TOT = pltpu.VMEM((8, HEADS * TOK), F32)


def params(mib):
    return pltpu.CompilerParams(vmem_limit_bytes=mib * MIB)


def cost(keys):
    rows = HEADS * TOK
    return pl.CostEstimate(
        flops=8 * rows * keys * HD, bytes_accessed=MIB, transcendentals=rows * keys
    )


def layout(keys):
    return [pltpu.VMEM((keys, 2 * HD), BF16), pltpu.VMEM((HD, keys), BF16)]


def chip(array):
    return pltpu.with_memory_space_constraint(array, pltpu.VMEM)


def hbm(array):
    return pltpu.with_memory_space_constraint(array, pltpu.HBM)


def permute(block, pairs):
    return lax.ppermute(block, AXES, pairs)


def shift_row(block):
    return permute(block, [(i, i + ROW) for i in range(DEVICES - ROW)])


def swap(block):
    return permute(block, [(i, i ^ 1) for i in range(DEVICES)])


def pack(keys, values):
    return pl.pallas_call(
        pack_kernel,
        out_shape=pltpu.VMEM((2 * TOK, HD), BF16),
        in_specs=[ANY, ANY],
        out_specs=VMEM,
        scratch_shapes=[pltpu.SemaphoreType.DMA((2,))],
        compiler_params=params(4),
        name="pack",
    )(hbm(keys), hbm(values))


def own_part(queries, own, doc_lengths):
    return pl.pallas_call(
        own_kernel,
        out_shape=(
            QT, ACC, TOT, pltpu.VMEM((1, M), jnp.int32), jax.ShapeDtypeStruct((1,), jnp.int32)
        ),
        in_specs=[ANY, ANY, VMEM],
        out_specs=(VMEM, VMEM, VMEM, VMEM, SMEM),
        scratch_shapes=[
            pltpu.VMEM((TOK, M), F32),
            pltpu.VMEM(queries.shape, BF16),
            pltpu.SMEM((NDOCS,), jnp.int32),
            pltpu.SemaphoreType.DMA((GROUPS,)),
            pltpu.SemaphoreType.DMA,
        ],
        compiler_params=params(16),
        cost_estimate=cost(TOK),
        name="own",
    )(hbm(doc_lengths), hbm(queries), chip(own))


def add_part(kernel, name, keys, first, qt, blocks, acc, tot):
    at = 2 + len(blocks)
    return pl.pallas_call(
        kernel,
        out_shape=(ACC, TOT),
        in_specs=[SMEM] + [VMEM] * (3 + len(blocks)),
        out_specs=(VMEM, VMEM),
        scratch_shapes=layout(keys),
        input_output_aliases={at: 0, at + 1: 1},
        compiler_params=params(28),
        cost_estimate=cost(keys),
        name=name,
    )(first, *[chip(a) for a in (qt, *blocks, acc, tot)])


def last_part(first, arrays, shape):
    return pl.pallas_call(
        last_kernel,
        out_shape=jax.ShapeDtypeStruct(shape, BF16),
        in_specs=[SMEM] + [VMEM] * len(arrays),
        out_specs=pl.BlockSpec(memory_space=pl.ANY),
        scratch_shapes=layout(6 * TOK)
        + [
            pltpu.VMEM((2, TOK, GROUP * HD), BF16),
            pltpu.VMEM((16, 2 * TOK, HD), BF16),
            pltpu.SemaphoreType.DMA((2,)),
        ],
        compiler_params=params(36),
        cost_estimate=cost(6 * TOK),
        name="last",
    )(first, *[chip(x) for x in arrays])


def shards(queries, keys, values, doc_lengths):
    col = lax.axis_index("inner") % ROW // 2
    own = pack(keys, values)

    z = shift_row(own)
    x = permute(own, [(i, i + 1) for i in range(0, DEVICES, 2)]
                + [(i, i + 15) for i in range(1, DEVICES - 15, 2)])
    own, z = lax.optimization_barrier((own, z))

    near = []
    for s in (1, 3, 2):
        message = jnp.where(col + s < ROW // 2, own, z)
        route = [(i, i // ROW * ROW + (i + 2 * s) % ROW) for i in range(DEVICES)]
        near.append(permute(message, route))
    z2 = swap(z)
    qt, acc, tot, begin, first = own_part(queries, own, doc_lengths)

    near = jnp.concatenate([near[0], near[2], near[1]], 0)
    near, acc, tot = lax.optimization_barrier((near, acc, tot))
    far = shift_row(near)
    near2 = swap(near)
    acc, tot = add_part(z_kernel, "zpart", 3 * TOK, first, qt, (z, z2, x), acc, tot)
    acc, tot = add_part(near_kernel, "nearpart", 6 * TOK, first, qt, (near, near2), acc, tot)
    far2 = swap(far)
    arrays = (qt, x, far, far2, near, near2, z, z2, own, begin, acc, tot)
    return last_part(first, arrays, queries.shape)


def solution(mesh):
    rows = P(AXES, None)
    return jax.shard_map(
        shards, mesh=mesh, in_specs=(rows, rows, rows, P()), out_specs=rows, check_vma=False
    )
```

```python
import functools

import jax
import jax.numpy as jnp
from jax import lax
from jax.experimental import pallas as pl
from jax.experimental.pallas import tpu as pltpu
from jax.sharding import PartitionSpec as P

AXES = ("outer", "inner")
ROW = 8
TOK = 320
HD = 128
HEADS = 16
GROUP = 4
GROUPS = HEADS // GROUP
M = GROUP * TOK
NDOCS = 64
DEVICES = 128
SCALE = 1.4426950408889634 / HD**0.5
NEVER = -1e30
NEW, OLD, THIRD = [pl.ds(i * 2 * TOK, 2 * TOK) for i in range(3)]
F32 = jnp.float32
BF16 = jnp.bfloat16
MIB = 2**20


def place():
    device = lax.axis_index("outer") * 64 + lax.axis_index("inner")
    return device, lax.rem(device, 2)


def columns(g, width=M):
    return pl.ds(g * width if isinstance(g, int) else pl.multiple_of(g * width, width), width)


def dot(a, b):
    return jnp.dot(a, b, preferred_element_type=F32)


def fold(p):
    return functools.reduce(lambda a, b: a + b, [p[i : i + 8] for i in range(0, p.shape[0], 8)])


def causal(begin):
    key = lax.broadcasted_iota(jnp.int32, (TOK, TOK), 0)
    row = lax.broadcasted_iota(jnp.int32, (TOK, TOK), 1)
    return jnp.where((key <= row) & (key >= begin), F32(0), F32(NEVER))


def pack_kernel(k_hbm, v_hbm, kv_ref, sems):
    copies = [
        pltpu.make_async_copy(half, kv_ref.at[pl.ds(i * TOK, TOK)], sems.at[i])
        for i, half in enumerate((k_hbm, v_hbm))
    ]
    for copy in copies:
        copy.start()
    for copy in copies:
        copy.wait()


def own_kernel(
    docs_hbm, q_hbm, kv_ref, qt_ref, acc_ref, tot_ref, begin_ref, first_ref,
    bias_ref, q_ref, docs, sems, docs_sem,
):
    read_docs = pltpu.make_async_copy(docs_hbm, docs, docs_sem)
    read_docs.start()

    def read(g):
        wide = columns(g, GROUP * HD)
        return pltpu.make_async_copy(q_hbm.at[:, wide], q_ref.at[:, wide], sems.at[g])

    for g in range(GROUPS):
        read(g).start()
    read_docs.wait()
    device, _ = place()
    token = lax.broadcasted_iota(jnp.int32, (1, TOK), 1)
    end = -device * TOK
    first = end
    begin = jnp.full((1, TOK), end, jnp.int32)
    for i in range(NDOCS):
        end = end + docs[i]
        begin = jnp.where(end <= token, end, begin)
        first = jnp.where(end <= 0, end, first)
    first_ref[0] = first
    begin_ref[...] = jnp.concatenate([begin] * GROUP, 1)
    bias_ref[...] = jnp.concatenate([causal(begin)] * GROUP, 1)
    qt_ref[HD:, :] = jnp.zeros((HD, HEADS * TOK), BF16)
    k = kv_ref[:TOK]
    vt = kv_ref[TOK:].T
    wide = 2

    for c in range(GROUPS // wide):
        for i in range(wide):
            read(c * wide + i).wait()
        heads = [q_ref[:, columns(c * wide * GROUP + i, HD)] for i in range(wide * GROUP)]
        qt = jnp.concatenate(heads, 0).T
        at = columns(c, wide * M)
        qt_ref[:HD, at] = qt
        s = dot(k, qt) + jnp.concatenate([bias_ref[...]] * wide, 1)
        m = jnp.max(s, 0, keepdims=True)
        p = jnp.exp2((s - m) * SCALE)
        tot_ref[:, at] = fold(p)
        acc_ref[:, at] = dot(vt, p.astype(BF16))
        begins = jnp.concatenate([begin_ref[...]] * wide, 1)
        shift = jnp.where(begins < 0, -m, F32(NEVER))
        line = lax.broadcasted_iota(jnp.int32, (16, wide * M), 0)
        extra = jnp.where(line == 3, F32(1), F32(0))
        for i in range(3):
            part = shift.astype(BF16).astype(F32)
            extra = jnp.where(line == i, part, extra)
            shift = shift - part
        qt_ref[HD : HD + 16, at] = extra.astype(BF16)


def fill(blocks, first, k_ref, vt_ref):
    for i, (block, position) in enumerate(blocks):
        rows = slice(i * TOK, (i + 1) * TOK)
        k_ref[rows, :HD] = block[:TOK]
        key = lax.broadcasted_iota(jnp.int32, (TOK, HD), 0) + position
        lane = lax.broadcasted_iota(jnp.int32, (TOK, HD), 1)
        late = jnp.where(key >= first, F32(0), F32(NEVER))
        bias = jnp.where(lane < 3, F32(1), jnp.where(lane == 3, late, F32(0)))
        k_ref[rows, HD:] = bias.astype(BF16)
    vt_ref[...] = jnp.concatenate([block[TOK:] for block, _ in blocks], 0).T


def pair(ours, theirs, step, side):
    return [(ours, step * TOK), (theirs, (step + side) * TOK)]


def partial(g, qt_ref, k_ref, vt_ref):
    p = jnp.exp2(dot(k_ref[...], qt_ref[:, columns(g)]) * SCALE)
    return dot(vt_ref[...], p.astype(BF16)), fold(p)


def first_keys(k_ref, vt_ref, blocks):
    keys = len(blocks) * TOK
    return k_ref.at[pl.ds(0, keys)], vt_ref.at[:, pl.ds(0, keys)]


def add_all(need, blocks, qt_ref, acc_in, tot_in, acc, tot, first, k_ref, vt_ref):
    @pl.when(need)
    def _():
        fill(blocks, first, k_ref, vt_ref)

        @pl.loop(0, GROUPS)
        def _(g):
            a, t = partial(g, qt_ref, k_ref, vt_ref)
            acc[:, columns(g)] = acc_in[:, columns(g)] + a
            tot[:, columns(g)] = tot_in[:, columns(g)] + t


def z_kernel(first_ref, qt_ref, z, z2, acc_in, tot_in, acc, tot, k_ref, vt_ref):
    _, core = place()
    first = first_ref[0]
    blocks = pair(z, z2, -8, 1 - 2 * core)
    add_all(first < -6 * TOK, blocks, qt_ref, acc_in, tot_in, acc, tot, first, k_ref, vt_ref)


def near_kernel(first_ref, qt_ref, n1, n3, mx, acc_in, tot_in, acc, tot, k_ref, vt_ref):
    _, core = place()
    first = first_ref[0]
    side = 1 - 2 * core
    blocks = pair(n1, mx.at[NEW], -2, side) + pair(n3, mx.at[OLD], -6, side)
    some = first < -4 * TOK
    state = (qt_ref, acc_in, tot_in, acc, tot, first)
    add_all(some, blocks, *state, k_ref, vt_ref)
    few = jnp.logical_not(some) & (first < 0)
    add_all(few, blocks[:2], *state, *first_keys(k_ref, vt_ref, blocks[:2]))


def far_kernel(
    first_ref, qt_ref, f1, f3, g, mx, acc_in, tot_in, acc, tot, k_ref, vt_ref, k1_ref, vt1_ref
):
    _, core = place()
    first = first_ref[0]
    side = 1 - 2 * core
    blocks = pair(f1, g.at[NEW], -10, side) + pair(f3, g.at[OLD], -14, side)
    blocks.append((mx.at[THIRD], jnp.where(core == 0, -15, -1) * TOK))
    some = first < -8 * TOK
    state = (qt_ref, acc_in, tot_in, acc, tot, first)
    add_all(some, blocks, *state, k_ref, vt_ref)
    few = jnp.logical_not(some) & (core == 1) & (first < 0)
    add_all(few, blocks[4:], *state, k1_ref, vt1_ref)


def last_kernel(
    first_ref, qt_ref, r2, t2, n1, n3, mx, f1, f3, fo, z, z2, own, begin_ref, acc, tot,
    out_hbm, k_ref, vt_ref, out_ref, window, sems,
):
    _, core = place()
    side = 1 - 2 * core
    first = first_ref[0]
    blocks = pair(r2.at[NEW], t2.at[NEW], -4, side) + pair(r2.at[OLD], t2.at[OLD], -12, side)
    some = first < -10 * TOK
    few = jnp.logical_not(some) & (first < -2 * TOK)
    half = first_keys(k_ref, vt_ref, blocks[:2])

    @pl.when(some)
    def _():
        fill(blocks, first, k_ref, vt_ref)

    @pl.when(few)
    def _():
        fill(blocks[:2], first, *half)

    def send(g):
        return pltpu.make_async_copy(
            out_ref.at[lax.rem(g, 2)], out_hbm.at[:, columns(g, GROUP * HD)], sems.at[lax.rem(g, 2)]
        )

    def put(g, result):
        for i in range(GROUP):
            part = result[:, i * TOK : (i + 1) * TOK].T
            out_ref[lax.rem(g, 2), :, i * HD : (i + 1) * HD] = part.astype(BF16)

    @pl.loop(0, GROUPS)
    def _(g):
        @pl.when(g >= 2)
        def _():
            send(g - 2).wait()

        def finish(a, t):
            total = jnp.sum(t, 0, keepdims=True)
            put(g, a / total)
            return jnp.max(total)

        def with_blocks(refs):
            a, t = partial(g, qt_ref, *refs)
            return finish(acc[:, columns(g)] + a, tot[:, columns(g)] + t)

        def without():
            return finish(acc[:, columns(g)], tot[:, columns(g)])

        largest = lax.cond(
            some,
            lambda: with_blocks((k_ref, vt_ref)),
            lambda: lax.cond(few, lambda: with_blocks(half), without),
        )

        @pl.when(jnp.logical_not(largest < F32(1e30)))
        def _():
            pieces = [(own, 0), (z, -8), (z2, side - 8), (mx.at[THIRD], jnp.where(core == 0, -15, -1))]
            for i, ours, theirs in (
                (-2, n1, mx.at[NEW]), (-6, n3, mx.at[OLD]), (-10, f1, fo.at[NEW]), (-14, f3, fo.at[OLD]),
                (-4, r2.at[NEW], t2.at[NEW]), (-12, r2.at[OLD], t2.at[OLD]),
            ):
                pieces += [(ours, i), (theirs, i + side)]
            for piece, step in pieces:
                window[step + 15] = piece[...]
            q = qt_ref[:HD, columns(g)]
            row = jnp.concatenate([lax.broadcasted_iota(jnp.int32, (1, TOK), 1)] * GROUP, 1)

            def step(i, carry):
                top, a, t = carry
                s = dot(window[15 - i, :TOK], q) * SCALE
                key = lax.broadcasted_iota(jnp.int32, (TOK, M), 0) - i * TOK
                keep = (key <= row) & (key >= begin_ref[...])
                s = jnp.where(keep, s, F32(NEVER))
                new = jnp.maximum(top, jnp.max(s, 0, keepdims=True))
                p = jnp.where(keep, jnp.exp2(s - new), F32(0))
                decay = jnp.exp2(top - new)
                return new, a * decay + dot(window[15 - i, TOK:].T, p.astype(BF16)), t * decay + fold(p)

            zero = (jnp.full((1, M), NEVER, F32), jnp.zeros((HD, M), F32), jnp.zeros((8, M), F32))
            _, a, t = lax.fori_loop(0, 16, step, zero)
            put(g, a / jnp.sum(t, 0, keepdims=True))

        send(g).start()

    for g in (GROUPS - 2, GROUPS - 1):
        send(g).wait()


VMEM = pl.BlockSpec(memory_space=pltpu.VMEM)
SMEM = pl.BlockSpec(memory_space=pltpu.SMEM)
ANY = pl.BlockSpec(memory_space=pl.ANY)
QT = pltpu.VMEM((2 * HD, HEADS * TOK), BF16)
ACC = pltpu.VMEM((HD, HEADS * TOK), F32)
TOT = pltpu.VMEM((8, HEADS * TOK), F32)


def params(mib):
    return pltpu.CompilerParams(vmem_limit_bytes=mib * MIB)


def cost(keys):
    rows = HEADS * TOK
    return pl.CostEstimate(
        flops=8 * rows * keys * HD, bytes_accessed=MIB, transcendentals=rows * keys
    )


def layout(keys):
    return [pltpu.VMEM((keys, 2 * HD), BF16), pltpu.VMEM((HD, keys), BF16)]


def chip(array):
    return pltpu.with_memory_space_constraint(array, pltpu.VMEM)


def hbm(array):
    return pltpu.with_memory_space_constraint(array, pltpu.HBM)


def permute(block, pairs):
    return lax.ppermute(block, AXES, pairs)


def shift_row(block):
    return permute(block, [(i, (i + ROW) % DEVICES) for i in range(DEVICES)])


def swap(block):
    return permute(block, [(i, i ^ 1) for i in range(DEVICES)])


def pack(keys, values):
    return pl.pallas_call(
        pack_kernel,
        out_shape=pltpu.VMEM((2 * TOK, HD), BF16),
        in_specs=[ANY, ANY],
        out_specs=VMEM,
        scratch_shapes=[pltpu.SemaphoreType.DMA((2,))],
        compiler_params=params(4),
        name="pack",
    )(hbm(keys), hbm(values))


def own_part(queries, own, doc_lengths):
    return pl.pallas_call(
        own_kernel,
        out_shape=(
            QT, ACC, TOT, pltpu.VMEM((1, M), jnp.int32), jax.ShapeDtypeStruct((1,), jnp.int32)
        ),
        in_specs=[ANY, ANY, VMEM],
        out_specs=(VMEM, VMEM, VMEM, VMEM, SMEM),
        scratch_shapes=[
            pltpu.VMEM((TOK, M), F32),
            pltpu.VMEM(queries.shape, BF16),
            pltpu.SMEM((NDOCS,), jnp.int32),
            pltpu.SemaphoreType.DMA((GROUPS,)),
            pltpu.SemaphoreType.DMA,
        ],
        compiler_params=params(16),
        cost_estimate=cost(TOK),
        name="own",
    )(hbm(doc_lengths), hbm(queries), chip(own))


def add_part(kernel, name, keys, first, qt, blocks, acc, tot):
    at = 2 + len(blocks)
    return pl.pallas_call(
        kernel,
        out_shape=(ACC, TOT),
        in_specs=[SMEM] + [VMEM] * (3 + len(blocks)),
        out_specs=(VMEM, VMEM),
        scratch_shapes=layout(keys) + (layout(TOK) if name == "far" else []),
        input_output_aliases={at: 0, at + 1: 1},
        compiler_params=params(20),
        cost_estimate=cost(keys),
        name=name,
    )(first, *[chip(a) for a in (qt, *blocks, acc, tot)])


def last_part(first, arrays, shape):
    return pl.pallas_call(
        last_kernel,
        out_shape=jax.ShapeDtypeStruct(shape, BF16),
        in_specs=[SMEM] + [VMEM] * len(arrays),
        out_specs=pl.BlockSpec(memory_space=pl.ANY),
        scratch_shapes=layout(4 * TOK)
        + [
            pltpu.VMEM((2, TOK, GROUP * HD), BF16),
            pltpu.VMEM((16, 2 * TOK, HD), BF16),
            pltpu.SemaphoreType.DMA((2,)),
        ],
        compiler_params=params(28),
        cost_estimate=cost(4 * TOK),
        name="last",
    )(first, *[chip(x) for x in arrays])


def shards(queries, keys, values, doc_lengths):
    col = lax.axis_index("inner") % ROW // 2
    own = pack(keys, values)

    def around(s, *pairs):
        behind = col + s < ROW // 2
        message = [jnp.where(behind, recent, older) for recent, older in pairs]
        route = [(i, i // ROW * ROW + (i + 2 * s) % ROW) for i in range(DEVICES)]
        return permute(jnp.concatenate(message, 0), route)

    z = shift_row(own)
    qt, acc, tot, begin, first = own_part(queries, own, doc_lengths)
    z, acc, tot = lax.optimization_barrier((z, acc, tot))

    n1, n3 = around(1, (own, z)), around(3, (own, z))
    zz = shift_row(z)
    z2 = swap(z)
    acc, tot = add_part(z_kernel, "zpart", 2 * TOK, first, qt, (z, z2), acc, tot)

    n1, n3, zz, tot = lax.optimization_barrier((n1, n3, zz, tot))
    f1, f3 = around(1, (z, zz)), around(3, (z, zz))
    r2 = around(2, (own, z), (z, zz))
    x = jnp.where(lax.axis_index("inner") % 2 == 0, own, zz)
    mx = swap(jnp.concatenate([n1, n3, x], 0))
    acc, tot = add_part(near_kernel, "near", 4 * TOK, first, qt, (n1, n3, mx), acc, tot)

    f1, f3, tot = lax.optimization_barrier((f1, f3, tot))
    g = swap(jnp.concatenate([f1, f3], 0))
    acc, tot = add_part(far_kernel, "far", 5 * TOK, first, qt, (f1, f3, g, mx), acc, tot)

    r2, tot = lax.optimization_barrier((r2, tot))
    t2 = swap(r2)
    arrays = (qt, r2, t2, n1, n3, mx, f1, f3, g, z, z2, own, begin, acc, tot)
    return last_part(first, arrays, queries.shape)


def solution(mesh):
    rows = P(AXES, None)
    return jax.shard_map(
        shards, mesh=mesh, in_specs=(rows, rows, rows, P()), out_specs=rows, check_vma=False
    )
```

```python
import functools

import jax
import jax.numpy as jnp
from jax import lax
from jax.experimental import pallas as pl
from jax.experimental.pallas import tpu as pltpu
from jax.sharding import PartitionSpec as P

AXES = ("outer", "inner")
ROW = 8
TOK = 320
HD = 128
HEADS = 16
GROUP = 8
GROUPS = HEADS // GROUP
M = GROUP * TOK
NDOCS = 64
DEVICES = 128
SCALE = 1.4426950408889634 / HD**0.5
NEVER = -1e30
NEW, OLD, THIRD = [pl.ds(i * 2 * TOK, 2 * TOK) for i in range(3)]
F32 = jnp.float32
BF16 = jnp.bfloat16
MIB = 2**20


def place():
    device = lax.axis_index("outer") * 64 + lax.axis_index("inner")
    return device, lax.rem(device, 2)


def columns(g, width=M):
    return pl.ds(g * width if isinstance(g, int) else pl.multiple_of(g * width, width), width)


def dot(a, b):
    return jnp.dot(a, b, preferred_element_type=F32)


def fold(p):
    return functools.reduce(lambda a, b: a + b, [p[i : i + 8] for i in range(0, p.shape[0], 8)])


def causal(begin):
    key = lax.broadcasted_iota(jnp.int32, (TOK, TOK), 0)
    row = lax.broadcasted_iota(jnp.int32, (TOK, TOK), 1)
    return jnp.where((key <= row) & (key >= begin), F32(0), F32(NEVER))


def pack_kernel(k_hbm, v_hbm, kv_ref, sems):
    copies = [
        pltpu.make_async_copy(half, kv_ref.at[pl.ds(i * TOK, TOK)], sems.at[i])
        for i, half in enumerate((k_hbm, v_hbm))
    ]
    for copy in copies:
        copy.start()
    for copy in copies:
        copy.wait()


def own_kernel(
    docs_hbm, q_hbm, kv_ref, qt_ref, acc_ref, tot_ref, begin_ref, first_ref,
    bias_ref, q_ref, docs, sems, docs_sem,
):
    read_docs = pltpu.make_async_copy(docs_hbm, docs, docs_sem)
    read_docs.start()

    def read(g):
        wide = columns(g, GROUP * HD)
        return pltpu.make_async_copy(q_hbm.at[:, wide], q_ref.at[:, wide], sems.at[g])

    for g in range(GROUPS):
        read(g).start()
    read_docs.wait()
    device, _ = place()
    token = lax.broadcasted_iota(jnp.int32, (1, TOK), 1)
    end = -device * TOK
    first = end
    begin = jnp.full((1, TOK), end, jnp.int32)
    for i in range(NDOCS):
        end = end + docs[i]
        begin = jnp.where(end <= token, end, begin)
        first = jnp.where(end <= 0, end, first)
    first_ref[0] = first
    begin_ref[...] = jnp.concatenate([begin] * GROUP, 1)
    bias_ref[...] = jnp.concatenate([causal(begin)] * GROUP, 1)
    qt_ref[HD:, :] = jnp.zeros((HD, HEADS * TOK), BF16)
    k = kv_ref[:TOK]
    vt = kv_ref[TOK:].T
    wide = 1

    for c in range(GROUPS // wide):
        for i in range(wide):
            read(c * wide + i).wait()
        heads = [q_ref[:, columns(c * wide * GROUP + i, HD)] for i in range(wide * GROUP)]
        qt = jnp.concatenate(heads, 0).T
        at = columns(c, wide * M)
        qt_ref[:HD, at] = qt
        s = dot(k, qt) + jnp.concatenate([bias_ref[...]] * wide, 1)
        m = jnp.max(s, 0, keepdims=True)
        p = jnp.exp2((s - m) * SCALE)
        tot_ref[:, at] = fold(p)
        acc_ref[:, at] = dot(vt, p.astype(BF16))
        begins = jnp.concatenate([begin_ref[...]] * wide, 1)
        shift = jnp.where(begins < 0, -m, F32(NEVER))
        line = lax.broadcasted_iota(jnp.int32, (16, wide * M), 0)
        extra = jnp.where(line == 3, F32(1), F32(0))
        for i in range(3):
            part = shift.astype(BF16).astype(F32)
            extra = jnp.where(line == i, part, extra)
            shift = shift - part
        qt_ref[HD : HD + 16, at] = extra.astype(BF16)


def fill(blocks, first, k_ref, vt_ref):
    for i, (block, position) in enumerate(blocks):
        rows = slice(i * TOK, (i + 1) * TOK)
        k_ref[rows, :HD] = block[:TOK]
        key = lax.broadcasted_iota(jnp.int32, (TOK, HD), 0) + position
        lane = lax.broadcasted_iota(jnp.int32, (TOK, HD), 1)
        late = jnp.where(key >= first, F32(0), F32(NEVER))
        bias = jnp.where(lane < 3, F32(1), jnp.where(lane == 3, late, F32(0)))
        k_ref[rows, HD:] = bias.astype(BF16)
    vt_ref[...] = jnp.concatenate([block[TOK:] for block, _ in blocks], 0).T


def pair(ours, theirs, step, side):
    return [(ours, step * TOK), (theirs, (step + side) * TOK)]


def partial(g, qt_ref, k_ref, vt_ref):
    p = jnp.exp2(dot(k_ref[...], qt_ref[:, columns(g)]) * SCALE)
    return dot(vt_ref[...], p.astype(BF16)), fold(p)


def first_keys(k_ref, vt_ref, blocks):
    keys = len(blocks) * TOK
    return k_ref.at[pl.ds(0, keys)], vt_ref.at[:, pl.ds(0, keys)]


def add_all(need, blocks, qt_ref, acc_in, tot_in, acc, tot, first, k_ref, vt_ref):
    @pl.when(need)
    def _():
        fill(blocks, first, k_ref, vt_ref)

        @pl.loop(0, GROUPS)
        def _(g):
            a, t = partial(g, qt_ref, k_ref, vt_ref)
            acc[:, columns(g)] = acc_in[:, columns(g)] + a
            tot[:, columns(g)] = tot_in[:, columns(g)] + t


def z_kernel(first_ref, qt_ref, z, z2, acc_in, tot_in, acc, tot, k_ref, vt_ref):
    _, core = place()
    first = first_ref[0]
    blocks = pair(z, z2, -8, 1 - 2 * core)
    add_all(first < -6 * TOK, blocks, qt_ref, acc_in, tot_in, acc, tot, first, k_ref, vt_ref)


def near_kernel(first_ref, qt_ref, n1, n3, mx, acc_in, tot_in, acc, tot, k_ref, vt_ref):
    _, core = place()
    first = first_ref[0]
    side = 1 - 2 * core
    blocks = pair(n1, mx.at[NEW], -2, side) + pair(n3, mx.at[OLD], -6, side)
    some = first < -4 * TOK
    state = (qt_ref, acc_in, tot_in, acc, tot, first)
    add_all(some, blocks, *state, k_ref, vt_ref)
    few = jnp.logical_not(some) & (first < 0)
    add_all(few, blocks[:2], *state, *first_keys(k_ref, vt_ref, blocks[:2]))


def far_kernel(
    first_ref, qt_ref, f1, f3, g, mx, acc_in, tot_in, acc, tot, k_ref, vt_ref, k1_ref, vt1_ref
):
    _, core = place()
    first = first_ref[0]
    side = 1 - 2 * core
    blocks = pair(f1, g.at[NEW], -10, side) + pair(f3, g.at[OLD], -14, side)
    blocks.append((mx.at[THIRD], jnp.where(core == 0, -15, -1) * TOK))
    some = first < -8 * TOK
    state = (qt_ref, acc_in, tot_in, acc, tot, first)
    add_all(some, blocks, *state, k_ref, vt_ref)
    few = jnp.logical_not(some) & (core == 1) & (first < 0)
    add_all(few, blocks[4:], *state, k1_ref, vt1_ref)


def last_kernel(
    first_ref, qt_ref, r2, t2, n1, n3, mx, f1, f3, fo, z, z2, own, begin_ref, acc, tot,
    out_hbm, k_ref, vt_ref, out_ref, window, sems,
):
    _, core = place()
    side = 1 - 2 * core
    first = first_ref[0]
    blocks = pair(r2.at[NEW], t2.at[NEW], -4, side) + pair(r2.at[OLD], t2.at[OLD], -12, side)
    some = first < -10 * TOK
    few = jnp.logical_not(some) & (first < -2 * TOK)
    half = first_keys(k_ref, vt_ref, blocks[:2])

    @pl.when(some)
    def _():
        fill(blocks, first, k_ref, vt_ref)

    @pl.when(few)
    def _():
        fill(blocks[:2], first, *half)

    def send(g):
        return pltpu.make_async_copy(
            out_ref.at[lax.rem(g, 2)], out_hbm.at[:, columns(g, GROUP * HD)], sems.at[lax.rem(g, 2)]
        )

    def put(g, result):
        result = result.astype(BF16)
        for i in range(GROUP):
            part = result[:, i * TOK : (i + 1) * TOK].T
            out_ref[lax.rem(g, 2), :, i * HD : (i + 1) * HD] = part

    @pl.loop(0, GROUPS)
    def _(g):
        @pl.when(g >= 2)
        def _():
            send(g - 2).wait()

        def finish(a, t):
            total = jnp.sum(t, 0, keepdims=True)
            put(g, a / total)
            return jnp.max(total)

        def with_blocks(refs):
            a, t = partial(g, qt_ref, *refs)
            return finish(acc[:, columns(g)] + a, tot[:, columns(g)] + t)

        def without():
            return finish(acc[:, columns(g)], tot[:, columns(g)])

        largest = lax.cond(
            some,
            lambda: with_blocks((k_ref, vt_ref)),
            lambda: lax.cond(few, lambda: with_blocks(half), without),
        )

        @pl.when(jnp.logical_not(largest < F32(1e30)))
        def _():
            pieces = [(own, 0), (z, -8), (z2, side - 8), (mx.at[THIRD], jnp.where(core == 0, -15, -1))]
            for i, ours, theirs in (
                (-2, n1, mx.at[NEW]), (-6, n3, mx.at[OLD]), (-10, f1, fo.at[NEW]), (-14, f3, fo.at[OLD]),
                (-4, r2.at[NEW], t2.at[NEW]), (-12, r2.at[OLD], t2.at[OLD]),
            ):
                pieces += [(ours, i), (theirs, i + side)]
            for piece, step in pieces:
                window[step + 15] = piece[...]
            q = qt_ref[:HD, columns(g)]
            row = jnp.concatenate([lax.broadcasted_iota(jnp.int32, (1, TOK), 1)] * GROUP, 1)

            def step(i, carry):
                top, a, t = carry
                s = dot(window[15 - i, :TOK], q) * SCALE
                key = lax.broadcasted_iota(jnp.int32, (TOK, M), 0) - i * TOK
                keep = (key <= row) & (key >= begin_ref[...])
                s = jnp.where(keep, s, F32(NEVER))
                new = jnp.maximum(top, jnp.max(s, 0, keepdims=True))
                p = jnp.where(keep, jnp.exp2(s - new), F32(0))
                decay = jnp.exp2(top - new)
                return new, a * decay + dot(window[15 - i, TOK:].T, p.astype(BF16)), t * decay + fold(p)

            zero = (jnp.full((1, M), NEVER, F32), jnp.zeros((HD, M), F32), jnp.zeros((8, M), F32))
            _, a, t = lax.fori_loop(0, 16, step, zero)
            put(g, a / jnp.sum(t, 0, keepdims=True))

        send(g).start()

    for g in (GROUPS - 2, GROUPS - 1):
        send(g).wait()


VMEM = pl.BlockSpec(memory_space=pltpu.VMEM)
SMEM = pl.BlockSpec(memory_space=pltpu.SMEM)
ANY = pl.BlockSpec(memory_space=pl.ANY)
QT = pltpu.VMEM((2 * HD, HEADS * TOK), BF16)
ACC = pltpu.VMEM((HD, HEADS * TOK), F32)
TOT = pltpu.VMEM((8, HEADS * TOK), F32)


def params(mib):
    return pltpu.CompilerParams(vmem_limit_bytes=mib * MIB)


def cost(keys):
    rows = HEADS * TOK
    return pl.CostEstimate(
        flops=8 * rows * keys * HD, bytes_accessed=MIB, transcendentals=rows * keys
    )


def layout(keys):
    return [pltpu.VMEM((keys, 2 * HD), BF16), pltpu.VMEM((HD, keys), BF16)]


def chip(array):
    return pltpu.with_memory_space_constraint(array, pltpu.VMEM)


def smem(array):
    return pltpu.with_memory_space_constraint(array, pltpu.SMEM)


def hbm(array):
    return pltpu.with_memory_space_constraint(array, pltpu.HBM)


def permute(block, pairs):
    return lax.ppermute(block, AXES, pairs)


def shift_row(block):
    return permute(block, [(i, (i + ROW) % DEVICES) for i in range(DEVICES)])


def swap(block):
    return permute(block, [(i, i ^ 1) for i in range(DEVICES)])


def pack(keys, values):
    return pl.pallas_call(
        pack_kernel,
        out_shape=pltpu.VMEM((2 * TOK, HD), BF16),
        in_specs=[ANY, ANY],
        out_specs=VMEM,
        scratch_shapes=[pltpu.SemaphoreType.DMA((2,))],
        compiler_params=params(4),
        name="pack",
    )(hbm(keys), hbm(values))


def own_part(queries, own, doc_lengths):
    return pl.pallas_call(
        own_kernel,
        out_shape=(
            QT, ACC, TOT, pltpu.VMEM((1, M), jnp.int32), pltpu.SMEM((1,), jnp.int32)
        ),
        in_specs=[ANY, ANY, VMEM],
        out_specs=(VMEM, VMEM, VMEM, VMEM, SMEM),
        scratch_shapes=[
            pltpu.VMEM((TOK, M), F32),
            pltpu.VMEM(queries.shape, BF16),
            pltpu.SMEM((NDOCS,), jnp.int32),
            pltpu.SemaphoreType.DMA((GROUPS,)),
            pltpu.SemaphoreType.DMA,
        ],
        compiler_params=params(24),
        cost_estimate=cost(TOK),
        name="own",
    )(hbm(doc_lengths), hbm(queries), chip(own))


def add_part(kernel, name, keys, first, qt, blocks, acc, tot):
    at = 2 + len(blocks)
    return pl.pallas_call(
        kernel,
        out_shape=(ACC, TOT),
        in_specs=[SMEM] + [VMEM] * (3 + len(blocks)),
        out_specs=(VMEM, VMEM),
        scratch_shapes=layout(keys) + (layout(TOK) if name == "far" else []),
        input_output_aliases={at: 0, at + 1: 1},
        compiler_params=params(30),
        cost_estimate=cost(keys),
        name=name,
    )(smem(first), *[chip(a) for a in (qt, *blocks, acc, tot)])


def last_part(first, arrays, shape):
    return pl.pallas_call(
        last_kernel,
        out_shape=jax.ShapeDtypeStruct(shape, BF16),
        in_specs=[SMEM] + [VMEM] * len(arrays),
        out_specs=pl.BlockSpec(memory_space=pl.ANY),
        scratch_shapes=layout(4 * TOK)
        + [
            pltpu.VMEM((2, TOK, GROUP * HD), BF16),
            pltpu.VMEM((16, 2 * TOK, HD), BF16),
            pltpu.SemaphoreType.DMA((2,)),
        ],
        compiler_params=params(36),
        cost_estimate=cost(4 * TOK),
        name="last",
    )(smem(first), *[chip(x) for x in arrays])


def shards(queries, keys, values, doc_lengths):
    col = lax.axis_index("inner") % ROW // 2
    own = pack(keys, values)

    def around(s, *pairs):
        behind = col + s < ROW // 2
        message = [jnp.where(behind, recent, older) for recent, older in pairs]
        route = [(i, i // ROW * ROW + (i + 2 * s) % ROW) for i in range(DEVICES)]
        return permute(jnp.concatenate(message, 0), route)

    z = shift_row(own)
    qt, acc, tot, begin, first = own_part(queries, own, doc_lengths)
    z, acc, tot = lax.optimization_barrier((z, acc, tot))

    n1, n3 = around(1, (own, z)), around(3, (own, z))
    zz = shift_row(z)
    z2 = swap(z)
    acc, tot = add_part(z_kernel, "zpart", 2 * TOK, first, qt, (z, z2), acc, tot)

    n1, n3, zz, tot = lax.optimization_barrier((n1, n3, zz, tot))
    f1, f3 = around(1, (z, zz)), around(3, (z, zz))
    r2 = around(2, (own, z), (z, zz))
    x = jnp.where(lax.axis_index("inner") % 2 == 0, own, zz)
    mx = swap(jnp.concatenate([n1, n3, x], 0))
    acc, tot = add_part(near_kernel, "near", 4 * TOK, first, qt, (n1, n3, mx), acc, tot)

    f1, f3, tot = lax.optimization_barrier((f1, f3, tot))
    g = swap(jnp.concatenate([f1, f3], 0))
    acc, tot = add_part(far_kernel, "far", 5 * TOK, first, qt, (f1, f3, g, mx), acc, tot)

    r2, tot = lax.optimization_barrier((r2, tot))
    t2 = swap(r2)
    arrays = (qt, r2, t2, n1, n3, mx, f1, f3, g, z, z2, own, begin, acc, tot)
    return last_part(first, arrays, queries.shape)


def solution(mesh):
    rows = P(AXES, None)
    return jax.shard_map(
        shards, mesh=mesh, in_specs=(rows, rows, rows, P()), out_specs=rows, check_vma=False
    )
```

```python
import functools

import jax
import jax.numpy as jnp
from jax import lax
from jax.experimental import pallas as pl
from jax.experimental.pallas import tpu as pltpu
from jax.sharding import PartitionSpec as P

AXES = ("outer", "inner")
ROW = 8
TOK = 320
HD = 128
HEADS = 16
GROUP = 8
GROUPS = HEADS // GROUP
M = GROUP * TOK
NDOCS = 64
DEVICES = 128
SCALE = 1.4426950408889634 / HD**0.5
NEVER = -1e30
NEW, OLD, THIRD = [pl.ds(i * 2 * TOK, 2 * TOK) for i in range(3)]
F32 = jnp.float32
BF16 = jnp.bfloat16
MIB = 2**20


def place():
    device = lax.axis_index("outer") * 64 + lax.axis_index("inner")
    return device, lax.rem(device, 2)


def columns(g, width=M):
    return pl.ds(g * width if isinstance(g, int) else pl.multiple_of(g * width, width), width)


def dot(a, b):
    return jnp.dot(a, b, preferred_element_type=F32)


def fold(p):
    return functools.reduce(lambda a, b: a + b, [p[i : i + 8] for i in range(0, p.shape[0], 8)])


def causal(begin):
    key = lax.broadcasted_iota(jnp.int32, (TOK, TOK), 0)
    row = lax.broadcasted_iota(jnp.int32, (TOK, TOK), 1)
    return jnp.where((key <= row) & (key >= begin), F32(0), F32(NEVER))


def pack_kernel(k_hbm, v_hbm, kv_ref, sems):
    copies = [
        pltpu.make_async_copy(half, kv_ref.at[pl.ds(i * TOK, TOK)], sems.at[i])
        for i, half in enumerate((k_hbm, v_hbm))
    ]
    for copy in copies:
        copy.start()
    for copy in copies:
        copy.wait()


def own_kernel(
    docs_hbm, q_hbm, kv_ref, qt_ref, acc_ref, tot_ref, begin_ref, first_ref,
    bias_ref, q_ref, docs, sems, docs_sem,
):
    read_docs = pltpu.make_async_copy(docs_hbm, docs, docs_sem)
    read_docs.start()

    def read(g):
        wide = columns(g, GROUP * HD)
        return pltpu.make_async_copy(q_hbm.at[:, wide], q_ref.at[:, wide], sems.at[g])

    for g in range(GROUPS):
        read(g).start()
    read_docs.wait()
    device, _ = place()
    token = lax.broadcasted_iota(jnp.int32, (1, TOK), 1)
    end = -device * TOK
    first = end
    begin = jnp.full((1, TOK), end, jnp.int32)
    for i in range(NDOCS):
        end = end + docs[i]
        begin = jnp.where(end <= token, end, begin)
        first = jnp.where(end <= 0, end, first)
    first_ref[0] = first
    begin_ref[...] = jnp.concatenate([begin] * GROUP, 1)
    bias_ref[...] = jnp.concatenate([causal(begin)] * GROUP, 1)
    qt_ref[HD:, :] = jnp.zeros((HD, HEADS * TOK), BF16)
    k = kv_ref[:TOK]
    vt = kv_ref[TOK:].T
    wide = 1

    for c in range(GROUPS // wide):
        for i in range(wide):
            read(c * wide + i).wait()
        heads = [q_ref[:, columns(c * wide * GROUP + i, HD)] for i in range(wide * GROUP)]
        qt = jnp.concatenate(heads, 0).T
        at = columns(c, wide * M)
        qt_ref[:HD, at] = qt
        s = dot(k, qt) + jnp.concatenate([bias_ref[...]] * wide, 1)
        m = jnp.max(s, 0, keepdims=True)
        p = jnp.exp2((s - m) * SCALE)
        tot_ref[:, at] = fold(p)
        acc_ref[:, at] = dot(vt, p.astype(BF16))
        begins = jnp.concatenate([begin_ref[...]] * wide, 1)
        shift = jnp.where(begins < 0, -m, F32(NEVER))
        line = lax.broadcasted_iota(jnp.int32, (16, wide * M), 0)
        extra = jnp.where(line == 3, F32(1), F32(0))
        for i in range(3):
            part = shift.astype(BF16).astype(F32)
            extra = jnp.where(line == i, part, extra)
            shift = shift - part
        qt_ref[HD : HD + 16, at] = extra.astype(BF16)


def fill(blocks, first, k_ref, vt_ref):
    for i, (block, position) in enumerate(blocks):
        rows = slice(i * TOK, (i + 1) * TOK)
        k_ref[rows, :HD] = block[:TOK]
        key = lax.broadcasted_iota(jnp.int32, (TOK, HD), 0) + position
        lane = lax.broadcasted_iota(jnp.int32, (TOK, HD), 1)
        late = jnp.where(key >= first, F32(0), F32(NEVER))
        bias = jnp.where(lane < 3, F32(1), jnp.where(lane == 3, late, F32(0)))
        k_ref[rows, HD:] = bias.astype(BF16)
    vt_ref[...] = jnp.concatenate([block[TOK:] for block, _ in blocks], 0).T


def pair(ours, theirs, step, side):
    return [(ours, step * TOK), (theirs, (step + side) * TOK)]


def partial(g, qt_ref, k_ref, vt_ref):
    p = jnp.exp2(dot(k_ref[...], qt_ref[:, columns(g)]) * SCALE)
    return dot(vt_ref[...], p.astype(BF16)), fold(p)


def first_keys(k_ref, vt_ref, blocks):
    keys = len(blocks) * TOK
    return k_ref.at[pl.ds(0, keys)], vt_ref.at[:, pl.ds(0, keys)]


def add_all(need, blocks, qt_ref, acc_in, tot_in, acc, tot, first, k_ref, vt_ref):
    @pl.when(need)
    def _():
        fill(blocks, first, k_ref, vt_ref)

        @pl.loop(0, GROUPS)
        def _(g):
            a, t = partial(g, qt_ref, k_ref, vt_ref)
            acc[:, columns(g)] = acc_in[:, columns(g)] + a
            tot[:, columns(g)] = tot_in[:, columns(g)] + t


def z_kernel(first_ref, qt_ref, z, z2, acc_in, tot_in, acc, tot, k_ref, vt_ref):
    _, core = place()
    first = first_ref[0]
    blocks = pair(z, z2, -8, 1 - 2 * core)
    add_all(first < -6 * TOK, blocks, qt_ref, acc_in, tot_in, acc, tot, first, k_ref, vt_ref)


def near_kernel(first_ref, qt_ref, n1, n3, mx, acc_in, tot_in, acc, tot, k_ref, vt_ref):
    _, core = place()
    first = first_ref[0]
    side = 1 - 2 * core
    blocks = pair(n1, mx.at[NEW], -2, side) + [(n3, -6 * TOK)]
    some = first < -4 * TOK
    state = (qt_ref, acc_in, tot_in, acc, tot, first)
    add_all(some, blocks, *state, k_ref, vt_ref)
    few = jnp.logical_not(some) & (first < 0)
    add_all(few, blocks[:2], *state, *first_keys(k_ref, vt_ref, blocks[:2]))


def far_kernel(
    first_ref, qt_ref, f1, f3, g, mx, acc_in, tot_in, acc, tot, k_ref, vt_ref, k1_ref, vt1_ref
):
    _, core = place()
    first = first_ref[0]
    side = 1 - 2 * core
    blocks = pair(f1, g.at[NEW], -10, side) + pair(f3, g.at[OLD], -14, side)
    blocks.append((mx.at[OLD], (side - 6) * TOK))
    blocks.append((mx.at[THIRD], jnp.where(core == 0, -15, -1) * TOK))
    some = first < -8 * TOK
    state = (qt_ref, acc_in, tot_in, acc, tot, first)
    add_all(some, blocks, *state, k_ref, vt_ref)
    few = jnp.logical_not(some) & (first < jnp.where(core == 1, 0, -4) * TOK)
    add_all(few, blocks[4:], *state, k1_ref, vt1_ref)


def last_kernel(
    first_ref, qt_ref, r2, t2, n1, n3, mx, f1, f3, fo, z, z2, own, begin_ref, acc, tot,
    out_hbm, k_ref, vt_ref, out_ref, window, sems,
):
    _, core = place()
    side = 1 - 2 * core
    first = first_ref[0]
    blocks = pair(r2.at[NEW], t2.at[NEW], -4, side) + pair(r2.at[OLD], t2.at[OLD], -12, side)
    some = first < -10 * TOK
    few = jnp.logical_not(some) & (first < -2 * TOK)
    half = first_keys(k_ref, vt_ref, blocks[:2])

    @pl.when(some)
    def _():
        fill(blocks, first, k_ref, vt_ref)

    @pl.when(few)
    def _():
        fill(blocks[:2], first, *half)

    def send(g):
        return pltpu.make_async_copy(
            out_ref.at[lax.rem(g, 2)], out_hbm.at[:, columns(g, GROUP * HD)], sems.at[lax.rem(g, 2)]
        )

    def put(g, result):
        result = result.astype(BF16)
        for i in range(GROUP):
            part = result[:, i * TOK : (i + 1) * TOK].T
            out_ref[lax.rem(g, 2), :, i * HD : (i + 1) * HD] = part

    @pl.loop(0, GROUPS)
    def _(g):
        @pl.when(g >= 2)
        def _():
            send(g - 2).wait()

        def finish(a, t):
            total = jnp.sum(t, 0, keepdims=True)
            put(g, a / total)
            return jnp.max(total)

        def with_blocks(refs):
            a, t = partial(g, qt_ref, *refs)
            return finish(acc[:, columns(g)] + a, tot[:, columns(g)] + t)

        def without():
            return finish(acc[:, columns(g)], tot[:, columns(g)])

        largest = lax.cond(
            some,
            lambda: with_blocks((k_ref, vt_ref)),
            lambda: lax.cond(few, lambda: with_blocks(half), without),
        )

        @pl.when(jnp.logical_not(largest < F32(1e30)))
        def _():
            pieces = [(own, 0), (z, -8), (z2, side - 8), (mx.at[THIRD], jnp.where(core == 0, -15, -1))]
            for i, ours, theirs in (
                (-2, n1, mx.at[NEW]), (-6, n3, mx.at[OLD]), (-10, f1, fo.at[NEW]), (-14, f3, fo.at[OLD]),
                (-4, r2.at[NEW], t2.at[NEW]), (-12, r2.at[OLD], t2.at[OLD]),
            ):
                pieces += [(ours, i), (theirs, i + side)]
            for piece, step in pieces:
                window[step + 15] = piece[...]
            q = qt_ref[:HD, columns(g)]
            row = jnp.concatenate([lax.broadcasted_iota(jnp.int32, (1, TOK), 1)] * GROUP, 1)

            def step(i, carry):
                top, a, t = carry
                s = dot(window[15 - i, :TOK], q) * SCALE
                key = lax.broadcasted_iota(jnp.int32, (TOK, M), 0) - i * TOK
                keep = (key <= row) & (key >= begin_ref[...])
                s = jnp.where(keep, s, F32(NEVER))
                new = jnp.maximum(top, jnp.max(s, 0, keepdims=True))
                p = jnp.where(keep, jnp.exp2(s - new), F32(0))
                decay = jnp.exp2(top - new)
                return new, a * decay + dot(window[15 - i, TOK:].T, p.astype(BF16)), t * decay + fold(p)

            zero = (jnp.full((1, M), NEVER, F32), jnp.zeros((HD, M), F32), jnp.zeros((8, M), F32))
            _, a, t = lax.fori_loop(0, 16, step, zero)
            put(g, a / jnp.sum(t, 0, keepdims=True))

        send(g).start()

    for g in (GROUPS - 2, GROUPS - 1):
        send(g).wait()


VMEM = pl.BlockSpec(memory_space=pltpu.VMEM)
SMEM = pl.BlockSpec(memory_space=pltpu.SMEM)
ANY = pl.BlockSpec(memory_space=pl.ANY)
QT = pltpu.VMEM((2 * HD, HEADS * TOK), BF16)
ACC = pltpu.VMEM((HD, HEADS * TOK), F32)
TOT = pltpu.VMEM((8, HEADS * TOK), F32)


def params(mib):
    return pltpu.CompilerParams(vmem_limit_bytes=mib * MIB)


def cost(keys):
    rows = HEADS * TOK
    return pl.CostEstimate(
        flops=8 * rows * keys * HD, bytes_accessed=MIB, transcendentals=rows * keys
    )


def layout(keys):
    return [pltpu.VMEM((keys, 2 * HD), BF16), pltpu.VMEM((HD, keys), BF16)]


def chip(array):
    return pltpu.with_memory_space_constraint(array, pltpu.VMEM)


def smem(array):
    return pltpu.with_memory_space_constraint(array, pltpu.SMEM)


def hbm(array):
    return pltpu.with_memory_space_constraint(array, pltpu.HBM)


def permute(block, pairs):
    return lax.ppermute(block, AXES, pairs)


def shift_row(block):
    return permute(block, [(i, (i + ROW) % DEVICES) for i in range(DEVICES)])


def swap(block):
    return permute(block, [(i, i ^ 1) for i in range(DEVICES)])


def pack(keys, values):
    return pl.pallas_call(
        pack_kernel,
        out_shape=pltpu.VMEM((2 * TOK, HD), BF16),
        in_specs=[ANY, ANY],
        out_specs=VMEM,
        scratch_shapes=[pltpu.SemaphoreType.DMA((2,))],
        compiler_params=params(4),
        name="pack",
    )(hbm(keys), hbm(values))


def own_part(queries, own, doc_lengths):
    return pl.pallas_call(
        own_kernel,
        out_shape=(
            QT, ACC, TOT, pltpu.VMEM((1, M), jnp.int32), pltpu.SMEM((1,), jnp.int32)
        ),
        in_specs=[ANY, ANY, VMEM],
        out_specs=(VMEM, VMEM, VMEM, VMEM, SMEM),
        scratch_shapes=[
            pltpu.VMEM((TOK, M), F32),
            pltpu.VMEM(queries.shape, BF16),
            pltpu.SMEM((NDOCS,), jnp.int32),
            pltpu.SemaphoreType.DMA((GROUPS,)),
            pltpu.SemaphoreType.DMA,
        ],
        compiler_params=params(24),
        cost_estimate=cost(TOK),
        name="own",
    )(hbm(doc_lengths), hbm(queries), chip(own))


def add_part(kernel, name, keys, first, qt, blocks, acc, tot):
    at = 2 + len(blocks)
    return pl.pallas_call(
        kernel,
        out_shape=(ACC, TOT),
        in_specs=[SMEM] + [VMEM] * (3 + len(blocks)),
        out_specs=(VMEM, VMEM),
        scratch_shapes=layout(keys) + (layout(2 * TOK) if name == "far" else []),
        input_output_aliases={at: 0, at + 1: 1},
        compiler_params=params(36),
        cost_estimate=cost(keys),
        name=name,
    )(smem(first), *[chip(a) for a in (qt, *blocks, acc, tot)])


def last_part(first, arrays, shape):
    return pl.pallas_call(
        last_kernel,
        out_shape=jax.ShapeDtypeStruct(shape, BF16),
        in_specs=[SMEM] + [VMEM] * len(arrays),
        out_specs=pl.BlockSpec(memory_space=pl.ANY),
        scratch_shapes=layout(4 * TOK)
        + [
            pltpu.VMEM((2, TOK, GROUP * HD), BF16),
            pltpu.VMEM((16, 2 * TOK, HD), BF16),
            pltpu.SemaphoreType.DMA((2,)),
        ],
        compiler_params=params(36),
        cost_estimate=cost(4 * TOK),
        name="last",
    )(smem(first), *[chip(x) for x in arrays])


def shards(queries, keys, values, doc_lengths):
    col = lax.axis_index("inner") % ROW // 2
    own = pack(keys, values)

    def around(s, *pairs):
        behind = col + s < ROW // 2
        message = [jnp.where(behind, recent, older) for recent, older in pairs]
        route = [(i, i // ROW * ROW + (i + 2 * s) % ROW) for i in range(DEVICES)]
        return permute(jnp.concatenate(message, 0), route)

    z = shift_row(own)
    qt, acc, tot, begin, first = own_part(queries, own, doc_lengths)
    z, acc, tot = lax.optimization_barrier((z, acc, tot))

    n1, n3 = around(1, (own, z)), around(3, (own, z))
    zz = shift_row(z)
    z2 = swap(z)
    acc, tot = add_part(z_kernel, "zpart", 2 * TOK, first, qt, (z, z2), acc, tot)

    n1, n3, zz, tot = lax.optimization_barrier((n1, n3, zz, tot))
    f1, f3 = around(1, (z, zz)), around(3, (z, zz))
    r2 = around(2, (own, z), (z, zz))
    x = jnp.where(lax.axis_index("inner") % 2 == 0, own, zz)
    mx = swap(jnp.concatenate([n1, n3, x], 0))
    acc, tot = add_part(near_kernel, "near", 3 * TOK, first, qt, (n1, n3, mx), acc, tot)

    f1, f3, tot = lax.optimization_barrier((f1, f3, tot))
    g = swap(jnp.concatenate([f1, f3], 0))
    acc, tot = add_part(far_kernel, "far", 6 * TOK, first, qt, (f1, f3, g, mx), acc, tot)

    r2, tot = lax.optimization_barrier((r2, tot))
    t2 = swap(r2)
    arrays = (qt, r2, t2, n1, n3, mx, f1, f3, g, z, z2, own, begin, acc, tot)
    return last_part(first, arrays, queries.shape)


def solution(mesh):
    rows = P(AXES, None)
    return jax.shard_map(
        shards, mesh=mesh, in_specs=(rows, rows, rows, P()), out_specs=rows, check_vma=False
    )
```
